32 devices in a mesh: seq: 8 (over y, x, core), head: 4 (over z).
Axes of the slice: x: 2, y: 2, z: 4, core: 2. Of those that a mesh axis runs over, the one named last changes fastest.
Arguments:
- queries: bfloat16 [8192, 2048], P(('seq', 'head')), may hold values from -6 to 6
- keys_in: bfloat16 [8192, 2048], P(('seq', 'head')), may hold values from -6 to 6
- values_in: bfloat16 [8192, 2048], P(('seq', 'head')), may hold values from -6 to 6
- cotangent: bfloat16 [8192, 2048], P(('seq', 'head')), may hold values from -6 to 6
Outputs:
- attended: bfloat16 [8192, 2048], P(('seq', 'head'))
- grad_queries: bfloat16 [8192, 2048], P(('seq', 'head'))
- grad_keys: bfloat16 [8192, 2048], P(('seq', 'head'))
- grad_values: bfloat16 [8192, 2048], P(('seq', 'head'))
The draws below stay inside these ranges and needn't reach their ends.
All inputs are finite; a program needn't handle non-finite values.
Results may differ from the reference program's by a relative error of at most 0.029.
Values may be sent and summed in bfloat16 or wider, within the bound.
No kernel may reach another device: no remote copies, remote signals or barrier semaphores. Data moves between devices by JAX's collectives and lax.ppermute only.
A program may use at most 128 MiB of HBM per device.

```python
import math
import jax
import jax.numpy as jnp
from jax import lax

HEADS = 16
HEAD_DIM = 128
WIDTH = 2048
BLOCK = 128
SUMMARY = 8
SEQ_LEN = 8192
NKEYS = 512


def base_field(key):
    return jnp.clip(jax.random.normal(key, (SEQ_LEN, HEADS, HEAD_DIM), jnp.float32), -6.0, 6.0)


def draw_queries(key, part):
    field = base_field(jax.random.fold_in(key, 11))
    return field.reshape(SEQ_LEN, WIDTH).astype(jnp.bfloat16)


def draw_keys_in(key, part):
    field = base_field(jax.random.fold_in(key, 12))
    return field.reshape(SEQ_LEN, WIDTH).astype(jnp.bfloat16)


def block_levels(rng, dims, cuts, least, largest):
    level = 1.0
    for dim, parts in cuts:
        steps = jax.random.uniform(jax.random.fold_in(jax.random.fold_in(rng, 6), dim), (parts,), jnp.float32, least / len(cuts), largest / len(cuts))
        level = level * jnp.repeat(jnp.exp(steps), dims[dim] // parts).reshape((-1,) + (1,) * (len(dims) - 1 - dim))
    return level


def normal_values(stream_key, shape, deviation, reach, cuts=(), kind=jnp.bfloat16):
    result = jax.random.normal(stream_key, shape, jnp.float32) * deviation
    if len(cuts) > 0:
        result = block_levels(stream_key, shape, cuts, -0.22, 0.18) * result
    return jnp.clip(result, min=-reach, max=reach).astype(kind)


def setup_inputs(seed: int = 0) -> dict:
    splits = jax.random.split(jax.random.key(seed), 5)
    queries = draw_queries(jax.random.fold_in(splits[4], 71), 0)
    keys_in = draw_keys_in(jax.random.fold_in(splits[4], 71), 0)
    values_in = normal_values(splits[2], (SEQ_LEN, WIDTH), 1.0, 6.0, ((0, 32),))
    cotangent = normal_values(splits[3], (SEQ_LEN, WIDTH), 1.0, 6.0, ((0, 32),))
    return dict(queries=queries, keys_in=keys_in, values_in=values_in, cotangent=cotangent)


neg_fill = -1e+30

def rounded(matrix):
    return lax.optimization_barrier(matrix.astype(jnp.bfloat16)).astype(jnp.float32)

def reference(queries, keys_in, values_in, cotangent):
    scaling = 1.0 / math.sqrt(HEAD_DIM)
    nblocks = SEQ_LEN // BLOCK
    block_shape = (nblocks, BLOCK, HEADS, HEAD_DIM)
    query_blocks = queries.reshape(block_shape)
    key_blocks = keys_in.reshape(block_shape)
    value_blocks = values_in.reshape(block_shape)
    grad_blocks = cotangent.reshape(block_shape)
    key_rows = key_blocks[:, BLOCK - SUMMARY:].reshape(NKEYS, HEADS, HEAD_DIM).astype(jnp.float32)
    value_rows = value_blocks[:, BLOCK - SUMMARY:].reshape(NKEYS, HEADS, HEAD_DIM).astype(jnp.float32)
    key_block = jnp.arange(NKEYS, dtype=jnp.int32) // SUMMARY
    causal = jnp.arange(BLOCK, dtype=jnp.int32)[:, None] >= jnp.arange(BLOCK, dtype=jnp.int32)[None, :]

    def block_turn(carried, block_data):
        key_sum, value_sum = carried
        query_b, key_b, value_b, grad_b, block_index = block_data
        query_f = query_b.astype(jnp.float32)
        key_f = key_b.astype(jnp.float32)
        value_f = value_b.astype(jnp.float32)
        grad_f = grad_b.astype(jnp.float32)
        seen = (key_block < block_index)[None, None, :]
        local_scores = jnp.einsum('ihe,jhe->hij', query_f, key_f) * scaling
        summary_scores = jnp.einsum('ihe,jhe->hij', query_f, key_rows) * scaling
        highest = jnp.maximum(lax.optimization_barrier(jnp.max(jnp.where(causal, local_scores, neg_fill), axis=-1)), lax.optimization_barrier(jnp.max(jnp.where(seen, summary_scores, neg_fill), axis=-1)))
        norm_sum = lax.optimization_barrier(jnp.sum(jnp.where(causal, jnp.exp(local_scores - highest[..., None]), 0.0), axis=-1))
        norm_sum = norm_sum + lax.optimization_barrier(jnp.sum(jnp.where(seen, jnp.exp(summary_scores - highest[..., None]), 0.0), axis=-1))
        log_norm = highest + jnp.log(norm_sum)
        local_probs = jnp.where(causal, jnp.exp(local_scores - log_norm[..., None]), 0.0)
        summary_probs = jnp.where(seen, jnp.exp(summary_scores - log_norm[..., None]), 0.0)
        local_pb = rounded(local_probs)
        summary_pb = rounded(summary_probs)
        output = jnp.einsum('hij,jhe->ihe', local_pb, value_f) + jnp.einsum('hij,jhe->ihe', summary_pb, value_rows)
        output = rounded(output)
        delta = lax.optimization_barrier(jnp.sum(grad_f * output, axis=-1)).T
        local_ds = rounded(local_probs * (jnp.einsum('ihe,jhe->hij', grad_f, value_f) - delta[..., None]))
        summary_ds = rounded(summary_probs * (jnp.einsum('ihe,jhe->hij', grad_f, value_rows) - delta[..., None]))
        grad_query = (jnp.einsum('hij,jhe->ihe', local_ds, key_f) + jnp.einsum('hij,jhe->ihe', summary_ds, key_rows)) * scaling
        grad_key = jnp.einsum('hij,ihe->jhe', local_ds, query_f) * scaling
        grad_value = jnp.einsum('hij,ihe->jhe', local_pb, grad_f)
        key_sum = key_sum + jnp.einsum('hij,ihe->jhe', summary_ds, query_f) * scaling
        value_sum = value_sum + jnp.einsum('hij,ihe->jhe', summary_pb, grad_f)
        return ((key_sum, value_sum), (output, grad_query, grad_key, grad_value))
    start_sums = (jnp.zeros((NKEYS, HEADS, HEAD_DIM), jnp.float32), jnp.zeros((NKEYS, HEADS, HEAD_DIM), jnp.float32))
    block_ids = jnp.arange(nblocks, dtype=jnp.int32)
    (key_sum, value_sum), results = lax.scan(block_turn, start_sums, (query_blocks, key_blocks, value_blocks, grad_blocks, block_ids))
    output, grad_query, grad_key, grad_value = results
    key_extra = key_sum.reshape(nblocks, SUMMARY, HEADS, HEAD_DIM)
    value_extra = value_sum.reshape(nblocks, SUMMARY, HEADS, HEAD_DIM)
    grad_key = jnp.concatenate([grad_key[:, :BLOCK - SUMMARY], grad_key[:, BLOCK - SUMMARY:] + key_extra], axis=1)
    grad_value = jnp.concatenate([grad_value[:, :BLOCK - SUMMARY], grad_value[:, BLOCK - SUMMARY:] + value_extra], axis=1)
    attended = output.reshape(SEQ_LEN, WIDTH).astype(jnp.bfloat16)
    grad_queries = grad_query.reshape(SEQ_LEN, WIDTH).astype(jnp.bfloat16)
    grad_keys = grad_key.reshape(SEQ_LEN, WIDTH).astype(jnp.bfloat16)
    grad_values = grad_value.reshape(SEQ_LEN, WIDTH).astype(jnp.bfloat16)
    return (attended, grad_queries, grad_keys, grad_values)
```

```python
import functools
import math

import jax
import jax.numpy as jnp
from jax import lax
from jax.experimental import pallas as pl
from jax.experimental.pallas import tpu as pltpu
from jax.sharding import PartitionSpec as P

HEADS = 16
HEAD_DIM = 128
BLOCK = 128
SUMMARY = 8

neg_fill = -1e30
scaling = 1.0 / math.sqrt(HEAD_DIM)
chunk_heads = (8, 8)
vmem_bytes = 48 * 1024 * 1024


def dot(left, right, left_dim, right_dim):
    return lax.dot_general(
        left, right, (((left_dim,), (right_dim,)), ((), ())), preferred_element_type=jnp.float32
    )


def summary_rows(matrix, start, width):
    rows = [
        lax.slice(matrix, (b * BLOCK + BLOCK - SUMMARY, start), ((b + 1) * BLOCK, start + width))
        for b in range(matrix.shape[0] // BLOCK)
    ]
    return jnp.concatenate(rows, axis=0)


def attention_body(n_sum, n_cols, n_alias, *refs):
    q_ref, k_ref, v_ref, g_ref, local_bias, far_bias = refs[:6]
    col_refs = refs[6 : 6 + n_cols]
    out_refs = refs[6 + n_cols + n_alias :]
    o_ref, dq_ref, dk_ref, dv_ref, near_ref, own_ref, other_ref = out_refs
    q = q_ref[...]
    g = g_ref[...]
    k_loc = k_ref[...]
    v_loc = v_ref[...]
    n_loc = k_loc.shape[0]
    k_far = jnp.concatenate(
        [ref[j, :n_sum, :] for ref in col_refs for j in range(ref.shape[0])], axis=0
    )
    v_far = jnp.concatenate(
        [ref[j, n_sum:, :] for ref in col_refs for j in range(ref.shape[0])], axis=0
    )
    bias_far = far_bias[...]
    bias_far = jnp.concatenate([bias_far] * (q.shape[0] // bias_far.shape[1]), axis=1)
    s_loc = dot(k_loc, q, 1, 1) + local_bias[...]
    s_far = dot(k_far, q, 1, 1) + bias_far
    high = jnp.maximum(
        jnp.max(s_loc, axis=0, keepdims=True), jnp.max(s_far, axis=0, keepdims=True)
    )
    e_loc = jnp.exp((s_loc - high) * scaling)
    e_far = jnp.exp((s_far - high) * scaling)
    norm = jnp.sum(e_loc, axis=0, keepdims=True) + jnp.sum(e_far, axis=0, keepdims=True)
    inv = 1.0 / norm
    p_loc = e_loc * inv
    p_far = e_far * inv
    pb_loc = p_loc.astype(jnp.bfloat16)
    pb_far = p_far.astype(jnp.bfloat16)
    out_t = dot(v_loc, pb_loc, 0, 0) + dot(v_far, pb_far, 0, 0)
    out = out_t.T.astype(jnp.bfloat16)
    o_ref[...] = out
    g_t = g.astype(jnp.float32).T
    delta = jnp.sum(g_t * out_t.astype(jnp.bfloat16).astype(jnp.float32), axis=0, keepdims=True)
    ds_loc = (p_loc * (dot(v_loc, g, 1, 1) - delta)).astype(jnp.bfloat16)
    ds_far = (p_far * (dot(v_far, g, 1, 1) - delta)).astype(jnp.bfloat16)
    dq_t = dot(k_loc, ds_loc, 0, 0) + dot(k_far, ds_far, 0, 0)
    dq_ref[...] = (dq_t * scaling).T.astype(jnp.bfloat16)
    dk_loc = dot(ds_loc, q, 1, 0) * scaling
    dv_loc = dot(pb_loc, g, 1, 0)
    dk_ref[...] = dk_loc.astype(jnp.bfloat16)
    dv_ref[...] = dv_loc.astype(jnp.bfloat16)
    near = []
    for part in (dk_loc, dv_loc):
        for b in range(n_loc // BLOCK):
            near.append(part[(b + 1) * BLOCK - SUMMARY : (b + 1) * BLOCK, :])
    near_ref[...] = jnp.concatenate(near, axis=0)
    dk_far = (dot(ds_far, q, 1, 0) * scaling).astype(jnp.bfloat16)
    dv_far = dot(pb_far, g, 1, 0).astype(jnp.bfloat16)
    row = 0
    for half in (own_ref, other_ref):
        for c in range(half.shape[0]):
            for j in range(half.shape[1]):
                half[c, j, :n_sum, :] = dk_far[row : row + n_sum]
                half[c, j, n_sum:, :] = dv_far[row : row + n_sum]
                row += n_sum


def attention(q, k, v, g, local_bias, far_bias, cols, earlier, first, heads):
    tokens, width = q.shape
    n_cols = len(cols)
    nz, rows, chunk_width = cols[0].shape
    nkeys = far_bias.shape[0]
    head_spec = pl.BlockSpec((tokens, HEAD_DIM), lambda h: (0, first + h))
    col_spec = pl.BlockSpec((nz, rows, HEAD_DIM), lambda h: (0, 0, h))
    grads_shape = jax.ShapeDtypeStruct((n_cols // 2, nz, rows, chunk_width), jnp.bfloat16)
    grads_spec = pl.BlockSpec((n_cols // 2, nz, rows, HEAD_DIM), lambda h: (0, 0, 0, h))
    full = jax.ShapeDtypeStruct((tokens, width), jnp.bfloat16)
    return pl.pallas_call(
        functools.partial(attention_body, rows // 2, n_cols, len(earlier)),
        grid=(heads,),
        in_specs=[head_spec] * 4
        + [
            pl.BlockSpec(local_bias.shape, lambda h: (0, 0)),
            pl.BlockSpec(far_bias.shape, lambda h: (0, 0)),
        ]
        + [col_spec] * n_cols
        + [pl.BlockSpec(memory_space=pl.ANY)] * len(earlier),
        out_specs=[head_spec] * 4
        + [pl.BlockSpec((rows, HEAD_DIM), lambda h: (0, h)), grads_spec, grads_spec],
        out_shape=[full] * 4
        + [jax.ShapeDtypeStruct((rows, chunk_width), jnp.float32), grads_shape, grads_shape],
        input_output_aliases={6 + n_cols + i: i for i in range(len(earlier))},
        compiler_params=pltpu.CompilerParams(vmem_limit_bytes=vmem_bytes),
        cost_estimate=pl.CostEstimate(
            flops=heads * 12 * tokens * (tokens + nkeys) * HEAD_DIM,
            bytes_accessed=heads * HEAD_DIM * (16 * tokens + 8 * nkeys),
            transcendentals=heads * tokens * (tokens + nkeys),
        ),
        name="attention",
    )(q, k, v, g, local_bias, far_bias, *cols, *earlier)


def core_sum_body(own_ref, came_ref, *out_refs):
    for c, ref in enumerate(out_refs):
        total = own_ref[c].astype(jnp.float32) + came_ref[c].astype(jnp.float32)
        ref[...] = total.astype(ref.dtype)


def core_sum(own, came):
    n_cols = own.shape[0]
    shapes = [
        jax.ShapeDtypeStruct(own.shape[1:], jnp.float32 if c == 0 else jnp.bfloat16)
        for c in range(n_cols)
    ]
    return pl.pallas_call(
        core_sum_body,
        out_shape=shapes,
        compiler_params=pltpu.CompilerParams(vmem_limit_bytes=vmem_bytes),
        name="core_sum",
    )(own, came)


def column_sum_body(n_in, *refs):
    in_refs, out_refs = refs[:n_in], refs[n_in:]
    for j, ref in enumerate(out_refs):
        total = in_refs[0][j].astype(jnp.float32)
        for came in in_refs[1:]:
            total = total + came[j].astype(jnp.float32)
        ref[...] = total.astype(ref.dtype)


def column_sum(parts):
    nz = parts[0].shape[0]
    shapes = [
        jax.ShapeDtypeStruct(parts[0].shape[1:], jnp.float32 if j == 0 else jnp.bfloat16)
        for j in range(nz)
    ]
    return pl.pallas_call(
        functools.partial(column_sum_body, len(parts)),
        out_shape=shapes,
        compiler_params=pltpu.CompilerParams(vmem_limit_bytes=vmem_bytes),
        name="column_sum",
    )(*parts)


def finish_body(n_chunks, n_terms, n_blocks, *refs):
    dk_in, dv_in = refs[0], refs[1]
    terms = refs[2 : 2 + n_chunks * n_terms]
    dk_ref, dv_ref = refs[2 + n_chunks * n_terms :]
    totals = []
    for c in range(n_chunks):
        mine = terms[c * n_terms : (c + 1) * n_terms]
        total = mine[0][...]
        for term in mine[1:]:
            total = total + term[...].astype(jnp.float32)
        totals.append(total)
    total = jnp.concatenate(totals, axis=1)
    n_sum = total.shape[0] // 2
    block = pl.program_id(0)
    for half, (source, target) in enumerate(((dk_in, dk_ref), (dv_in, dv_ref))):
        fresh = total[half * n_sum : (half + 1) * n_sum]
        picked = fresh[:SUMMARY]
        for b in range(1, n_blocks):
            picked = jnp.where(block == b, fresh[b * SUMMARY : (b + 1) * SUMMARY], picked)
        kept = source[...].astype(jnp.float32)[: 16 - SUMMARY]
        target[...] = jnp.concatenate([kept, picked], axis=0).astype(jnp.bfloat16)


def finish(dk, dv, chunks):
    tokens, width = dk.shape
    n_blocks = tokens // BLOCK
    n_terms = len(chunks[0])
    edge = pl.BlockSpec((16, width), lambda b: (b * (BLOCK // 16) + BLOCK // 16 - 1, 0))
    terms = [term for chunk in chunks for term in chunk]
    return pl.pallas_call(
        functools.partial(finish_body, len(chunks), n_terms, n_blocks),
        grid=(n_blocks,),
        in_specs=[edge, edge] + [pl.BlockSpec(term.shape, lambda b: (0, 0)) for term in terms],
        out_specs=[edge, edge],
        out_shape=[jax.ShapeDtypeStruct(dk.shape, dk.dtype)] * 2,
        input_output_aliases={0: 0, 1: 1},
        compiler_params=pltpu.CompilerParams(vmem_limit_bytes=vmem_bytes),
        name="finish",
    )(dk, dv, *terms)


def on_device(n_seq, nz, queries, keys_in, values_in, cotangent):
    tokens = queries.shape[0]
    n_blocks = tokens // BLOCK
    n_sum = n_blocks * SUMMARY
    n_cols = n_seq // 2

    def flips(size, bits, keep):
        return [(i, i ^ bits) for i in range(size) if keep(i, i ^ bits)]

    def over_z(array, bits):
        return lax.ppermute(array, "head", flips(nz, bits, lambda a, b: True))

    def over_columns(array, bits, keep):
        return lax.ppermute(array, "seq", flips(n_seq, 2 * bits, keep))

    def over_core(array):
        return lax.ppermute(array, "seq", flips(n_seq, 1, lambda a, b: True))

    seq_pos = lax.axis_index("seq")
    z_pos = lax.axis_index("head")
    here = seq_pos * nz + z_pos
    sources = []
    for core in range(2):
        for c in range(n_cols):
            for j in range(nz):
                sources.append((seq_pos ^ (2 * c + core)) * nz + (z_pos ^ j))
    seen = jnp.stack(sources) < here
    far_bias = jnp.where(jnp.repeat(seen, n_sum), 0.0, neg_fill).astype(jnp.float32)
    far_bias = jnp.broadcast_to(far_bias[:, None], (far_bias.shape[0], 128))
    key_row = lax.broadcasted_iota(jnp.int32, (tokens, tokens), 0)
    query_row = lax.broadcasted_iota(jnp.int32, (tokens, tokens), 1)
    same = (key_row // BLOCK == query_row // BLOCK) & (key_row <= query_row)
    earlier_block = (key_row // BLOCK < query_row // BLOCK) & (key_row % BLOCK >= BLOCK - SUMMARY)
    local_bias = jnp.where(same | earlier_block, 0.0, neg_fill).astype(jnp.float32)

    firsts = [sum(chunk_heads[:c]) for c in range(len(chunk_heads))]
    gathered = []
    for first, heads in zip(firsts, chunk_heads):
        width = heads * HEAD_DIM
        start = first * HEAD_DIM
        mine = jnp.concatenate(
            [summary_rows(keys_in, start, width), summary_rows(values_in, start, width)], axis=0
        )
        line = jnp.stack([mine] + [over_z(mine, j) for j in range(1, nz)])
        cols = [line] + [over_columns(line, c, lambda a, b: a < b) for c in range(1, n_cols)]
        cols = cols + [over_core(col) for col in cols]
        gathered.append(cols)

    results = ()
    chunks = []
    for cols, first, heads in zip(gathered, firsts, chunk_heads):
        *results, near, own, other = attention(
            queries, keys_in, values_in, cotangent, local_bias, far_bias, cols, results, first, heads
        )
        sums = core_sum(own, over_core(other))
        sums = [sums[0]] + [
            over_columns(sums[c], c, lambda a, b: a > b) for c in range(1, n_cols)
        ]
        sums = column_sum(sums)
        sums = [sums[0]] + [over_z(sums[j], j) for j in range(1, nz)]
        chunks.append([near] + sums)
    attended, grad_queries, dk, dv = results
    grad_keys, grad_values = finish(dk, dv, chunks)
    return (attended, grad_queries, grad_keys, grad_values)


def solution(mesh):
    spec = P(("seq", "head"), None)
    return jax.shard_map(
        functools.partial(on_device, mesh.shape["seq"], mesh.shape["head"]),
        mesh=mesh,
        in_specs=(spec,) * 4,
        out_specs=(spec,) * 4,
        check_vma=False,
    )
```

```python
import functools
import math

import jax
import jax.numpy as jnp
from jax import lax
from jax.experimental import pallas as pl
from jax.experimental.pallas import tpu as pltpu
from jax.sharding import PartitionSpec as P

HEADS = 16
HEAD_DIM = 128
BLOCK = 128
SUMMARY = 8
EDGE = 16

neg_fill = -1e30
scaling = 1.0 / math.sqrt(HEAD_DIM)
exponent = scaling / math.log(2.0)
chunk_heads = (8, 8)
unroll = 4
vmem_bytes = 40 * 1024 * 1024
in_vmem = pl.BlockSpec(memory_space=pltpu.VMEM)
in_hbm = pl.BlockSpec(memory_space=pltpu.HBM)
in_smem = pl.BlockSpec(memory_space=pltpu.SMEM)
token_shape = jax.ShapeDtypeStruct((8, 128), jnp.float32)
params = pltpu.CompilerParams(vmem_limit_bytes=vmem_bytes)


def dot(left, right, left_dim, right_dim):
    return lax.dot_general(
        left, right, (((left_dim,), (right_dim,)), ((), ())), preferred_element_type=jnp.float32
    )


def summary_rows(matrix, start, width):
    rows = [
        lax.slice(matrix, (b * BLOCK + BLOCK - SUMMARY, start), ((b + 1) * BLOCK, start + width))
        for b in range(matrix.shape[0] // BLOCK)
    ]
    return jnp.concatenate(rows, axis=0)


def block_mask():
    key = lax.broadcasted_iota(jnp.int32, (BLOCK, BLOCK), 1)
    query = lax.broadcasted_iota(jnp.int32, (BLOCK, BLOCK), 0)
    return jnp.where(key <= query, 0.0, neg_fill)


def far_mask(seq_pos, z_pos, n_cols, nz, n_sum, tokens):
    shape = (tokens, 2 * n_cols * nz * n_sum)
    row = lax.broadcasted_iota(jnp.int32, shape, 1)
    query = lax.broadcasted_iota(jnp.int32, shape, 0)
    piece = row // n_sum
    core = piece // (n_cols * nz)
    column = (piece // nz) % n_cols
    source = (seq_pos ^ (2 * column + core)) * nz + (z_pos ^ (piece % nz))
    mine = (piece == 0) & (row // SUMMARY < query // BLOCK)
    return jnp.where((source < seq_pos * nz + z_pos) | mine, 0.0, neg_fill)


def attention_body(n_sum, n_cols, n_skip, first, heads, *refs):
    place_ref = refs[0]
    sources = refs[1:5]
    col_refs = refs[5 : 5 + n_cols]
    targets = refs[5 + n_cols + n_skip : 9 + n_cols + n_skip]
    near_ref, own_ref, other_ref, token_ref = refs[9 + n_cols + n_skip : 13 + n_cols + n_skip]
    near_mask, away_mask, loads, stores, load_sem, store_sem = refs[13 + n_cols + n_skip :]
    tokens = sources[0].shape[0]
    nz = col_refs[0].shape[0]
    steps = heads // unroll
    span = unroll * HEAD_DIM

    def window(step):
        return pl.ds(pl.multiple_of(first * HEAD_DIM + step * span, HEAD_DIM), span)

    def load(step, i):
        return pltpu.make_async_copy(
            sources[i].at[:, window(step)], loads.at[step, i], load_sem.at[step, i]
        )

    def store(step, i):
        return pltpu.make_async_copy(
            stores.at[step, i], targets[i].at[:, window(step)], store_sem.at[step, i]
        )

    for step in range(steps):
        for i in range(4):
            load(step, i).start()
    blocks = [slice(b * BLOCK, (b + 1) * BLOCK) for b in range(tokens // BLOCK)]
    token_ref[...] = jnp.zeros(token_ref.shape, token_ref.dtype)
    near_mask[...] = jnp.concatenate([block_mask()] * len(blocks), axis=0)
    away_mask[...] = far_mask(place_ref[0], place_ref[1], n_cols // 2, nz, n_sum, tokens)

    def beside(parts):
        return jnp.concatenate(parts, axis=1)

    def head(step, at, to):
        q, k_loc, v_loc, g = (loads[step, i, :, at] for i in range(4))
        k_far = jnp.concatenate([ref[j, :n_sum, to] for ref in col_refs for j in range(nz)], axis=0)
        v_far = jnp.concatenate([ref[j, n_sum:, to] for ref in col_refs for j in range(nz)], axis=0)
        s_loc = jnp.concatenate([dot(q[b], k_loc[b], 1, 1) for b in blocks], axis=0) + near_mask[...]
        s_far = dot(q, k_far, 1, 1) + away_mask[...]
        high = jnp.maximum(
            jnp.max(s_loc, axis=1, keepdims=True), jnp.max(s_far, axis=1, keepdims=True)
        )
        e_loc = jnp.exp2((s_loc - high) * exponent)
        e_far = jnp.exp2((s_far - high) * exponent)
        norm = jnp.sum(e_loc, axis=1, keepdims=True) + jnp.sum(e_far, axis=1, keepdims=True)
        inv = 1.0 / norm
        eb_loc = e_loc.astype(jnp.bfloat16)
        eb_far = e_far.astype(jnp.bfloat16)
        out = jnp.concatenate([dot(eb_loc[b], v_loc[b], 1, 0) for b in blocks], axis=0) + dot(
            eb_far, v_far, 1, 0
        )
        out = (out * inv).astype(jnp.bfloat16)
        stores[step, 0, :, at] = out
        gf = g.astype(jnp.float32)
        delta = jnp.sum(gf * out.astype(jnp.float32), axis=1, keepdims=True)
        factor = inv * scaling
        t_loc = (jnp.concatenate([dot(g[b], v_loc[b], 1, 1) for b in blocks], axis=0) - delta) * factor
        t_far = (dot(g, v_far, 1, 1) - delta) * factor
        ds_loc = (eb_loc.astype(jnp.float32) * t_loc).astype(jnp.bfloat16)
        ds_far = (eb_far.astype(jnp.float32) * t_far).astype(jnp.bfloat16)
        dq = jnp.concatenate([dot(ds_loc[b], k_loc[b], 1, 0) for b in blocks], axis=0) + dot(
            ds_far, k_far, 1, 0
        )
        stores[step, 1, :, at] = dq.astype(jnp.bfloat16)
        gi = (gf * inv).astype(jnp.bfloat16)
        row = 0
        for target, left, right in ((2, ds_loc, q), (3, eb_loc, gi)):
            for b in blocks:
                part = dot(left[b], right[b], 0, 0)
                stores[step, target, b, at] = part.astype(jnp.bfloat16)
                near_ref[row : row + EDGE, to] = part[BLOCK - EDGE :, :]
                row += EDGE
        dk_far = dot(q, ds_far, 0, 0).astype(jnp.bfloat16).T
        dv_far = dot(gi, eb_far, 0, 0).astype(jnp.bfloat16).T
        row = 0
        for half in (own_ref, other_ref):
            for c in range(n_cols // 2):
                for j in range(nz):
                    half[c, j, :n_sum, to] = dk_far[row : row + n_sum]
                    half[c, j, n_sum:, to] = dv_far[row : row + n_sum]
                    row += n_sum

    def turn(step, carried):
        for i in range(4):
            load(step, i).wait()
        for u in range(unroll):
            to = pl.ds(pl.multiple_of(step * span + u * HEAD_DIM, HEAD_DIM), HEAD_DIM)
            head(step, slice(u * HEAD_DIM, (u + 1) * HEAD_DIM), to)
        for i in range(4):
            store(step, i).start()
        return carried

    lax.fori_loop(0, steps, turn, 0)
    for step in range(steps):
        for i in range(4):
            store(step, i).wait()


def attention(place, q, k, v, g, cols, earlier, after, first, heads):
    tokens, width = q.shape
    n_cols = len(cols)
    nz, rows, chunk_width = cols[0].shape
    nkeys = n_cols * nz * rows // 2
    n_blocks = tokens // BLOCK
    grads_shape = jax.ShapeDtypeStruct((n_cols // 2, nz, rows, chunk_width), jnp.bfloat16)
    full = jax.ShapeDtypeStruct((tokens, width), jnp.bfloat16)
    n_skip = len(earlier) + len(after)
    return pl.pallas_call(
        functools.partial(attention_body, rows // 2, n_cols, n_skip, first, heads),
        in_specs=[in_smem]
        + [in_hbm] * 4
        + [in_vmem] * n_cols
        + [in_hbm] * len(earlier)
        + [in_vmem] * len(after),
        out_specs=[in_hbm] * 4 + [in_vmem] * 4,
        out_shape=[full] * 4
        + [
            jax.ShapeDtypeStruct((2 * n_blocks * EDGE, chunk_width), jnp.float32),
            grads_shape,
            grads_shape,
            token_shape,
        ],
        scratch_shapes=[
            pltpu.VMEM((tokens, BLOCK), jnp.float32),
            pltpu.VMEM((tokens, nkeys), jnp.float32),
            pltpu.VMEM((heads // unroll, 4, tokens, unroll * HEAD_DIM), jnp.bfloat16),
            pltpu.VMEM((heads // unroll, 4, tokens, unroll * HEAD_DIM), jnp.bfloat16),
            pltpu.SemaphoreType.DMA((heads // unroll, 4)),
            pltpu.SemaphoreType.DMA((heads // unroll, 4)),
        ],
        input_output_aliases={5 + n_cols + i: i for i in range(len(earlier))},
        compiler_params=params,
        cost_estimate=pl.CostEstimate(
            flops=heads * 12 * tokens * (tokens + nkeys) * HEAD_DIM,
            bytes_accessed=heads * HEAD_DIM * (16 * tokens + 8 * nkeys),
            transcendentals=heads * tokens * (tokens + nkeys),
        ),
        name="attention",
    )(place, *[pltpu.with_memory_space_constraint(x, pltpu.HBM) for x in (q, k, v, g)], *cols, *earlier, *after)


def hold_body(*refs):
    pass


def hold(arrays, *after):
    return pl.pallas_call(
        hold_body,
        in_specs=[in_vmem] * (len(arrays) + len(after)),
        out_specs=[in_vmem] * len(arrays),
        out_shape=[jax.ShapeDtypeStruct(a.shape, a.dtype) for a in arrays],
        input_output_aliases={i: i for i in range(len(arrays))},
        compiler_params=params,
        name="hold",
    )(*arrays, *after)


def line_body(n_in, *refs):
    line_ref, token_ref = refs[-2:]
    for j in range(n_in):
        line_ref[j] = refs[j][...]
    token_ref[...] = jnp.zeros(token_ref.shape, token_ref.dtype)


def stack_line(pieces, *after):
    shape = (len(pieces),) + pieces[0].shape
    return pl.pallas_call(
        functools.partial(line_body, len(pieces)),
        in_specs=[in_vmem] * (len(pieces) + len(after)),
        out_specs=[in_vmem] * 2,
        out_shape=[jax.ShapeDtypeStruct(shape, pieces[0].dtype), token_shape],
        compiler_params=params,
        name="line",
    )(*pieces, *after)


def core_sum_body(own_ref, came_ref, *out_refs):
    token_ref = out_refs[-1]
    for c, ref in enumerate(out_refs[:-1]):
        total = own_ref[c].astype(jnp.float32) + came_ref[c].astype(jnp.float32)
        ref[...] = total.astype(ref.dtype)
    token_ref[...] = jnp.zeros(token_ref.shape, token_ref.dtype)


def core_sum(own, came):
    n_cols = own.shape[0]
    shapes = [
        jax.ShapeDtypeStruct(own.shape[1:], jnp.float32 if c == 0 else jnp.bfloat16)
        for c in range(n_cols)
    ]
    return pl.pallas_call(
        core_sum_body,
        in_specs=[in_vmem] * 2,
        out_specs=[in_vmem] * (n_cols + 1),
        out_shape=shapes + [token_shape],
        compiler_params=params,
        name="core_sum",
    )(own, came)


def column_sum_body(n_in, n_after, *refs):
    in_refs, out_refs = refs[:n_in], refs[n_in + n_after :]
    token_ref = out_refs[-1]
    for j, ref in enumerate(out_refs[:-1]):
        total = in_refs[0][j].astype(jnp.float32)
        for came in in_refs[1:]:
            total = total + came[j].astype(jnp.float32)
        ref[...] = total.astype(ref.dtype)
    token_ref[...] = jnp.zeros(token_ref.shape, token_ref.dtype)


def column_sum(parts, *after):
    nz = parts[0].shape[0]
    shapes = [
        jax.ShapeDtypeStruct(parts[0].shape[1:], jnp.float32 if j == 0 else jnp.bfloat16)
        for j in range(nz)
    ]
    return pl.pallas_call(
        functools.partial(column_sum_body, len(parts), len(after)),
        in_specs=[in_vmem] * (len(parts) + len(after)),
        out_specs=[in_vmem] * (nz + 1),
        out_shape=shapes + [token_shape],
        compiler_params=params,
        name="column_sum",
    )(*parts, *after)


def finish_body(n_chunks, n_terms, n_blocks, *refs):
    terms = refs[2 : 2 + n_chunks * n_terms]
    targets = refs[2 + n_chunks * n_terms : 4 + n_chunks * n_terms]
    edges, sem = refs[4 + n_chunks * n_terms :]
    at = 0
    for c in range(n_chunks):
        near, *mine = terms[c * n_terms : (c + 1) * n_terms]
        total = mine[0][...]
        for term in mine[1:]:
            total = total + term[...].astype(jnp.float32)
        to = pl.ds(at, near.shape[1])
        for row in range(2 * n_blocks):
            tile = near[row * EDGE : (row + 1) * EDGE, :]
            more = total[row * SUMMARY : (row + 1) * SUMMARY]
            edge = jnp.concatenate([tile[: EDGE - SUMMARY], tile[EDGE - SUMMARY :] + more], axis=0)
            edges[row, :, to] = edge.astype(jnp.bfloat16)
        at += near.shape[1]
    copies = [
        pltpu.make_async_copy(
            edges.at[row],
            targets[row // n_blocks].at[pl.ds((row % n_blocks + 1) * BLOCK - EDGE, EDGE), :],
            sem.at[row],
        )
        for row in range(2 * n_blocks)
    ]
    for copy in copies:
        copy.start()
    for copy in copies:
        copy.wait()


def finish(dk, dv, chunks):
    tokens, width = dk.shape
    n_blocks = tokens // BLOCK
    n_terms = len(chunks[0])
    terms = [term for chunk in chunks for term in chunk]
    anywhere = pl.BlockSpec(memory_space=pl.ANY)
    return pl.pallas_call(
        functools.partial(finish_body, len(chunks), n_terms, n_blocks),
        in_specs=[anywhere] * 2 + [in_vmem] * len(terms),
        out_specs=[anywhere] * 2,
        out_shape=[jax.ShapeDtypeStruct(dk.shape, dk.dtype)] * 2,
        scratch_shapes=[
            pltpu.VMEM((2 * n_blocks, EDGE, width), jnp.bfloat16),
            pltpu.SemaphoreType.DMA((2 * n_blocks,)),
        ],
        input_output_aliases={0: 0, 1: 1},
        compiler_params=params,
        name="finish",
    )(dk, dv, *terms)


def on_device(n_seq, nz, queries, keys_in, values_in, cotangent):
    n_cols = n_seq // 2

    def over_z(array, bits):
        return lax.ppermute(array, "head", [(i, i ^ bits) for i in range(nz)])

    def over_seq(array, bits):
        return lax.ppermute(array, "seq", [(i, i ^ bits) for i in range(n_seq)])

    def spread_z(piece):
        return [over_z(piece, j) for j in reversed(range(1, nz))][::-1]

    def spread_columns(line):
        return [over_seq(line, 2 * c) for c in reversed(range(1, n_cols))][::-1]

    place = jnp.stack([lax.axis_index("seq"), lax.axis_index("head")]).astype(jnp.int32)
    n_chunks = len(chunk_heads)
    firsts = [sum(chunk_heads[:c]) for c in range(n_chunks)]
    pieces = []
    for first, heads in zip(firsts, chunk_heads):
        width = heads * HEAD_DIM
        start = first * HEAD_DIM
        mine = jnp.concatenate(
            [summary_rows(keys_in, start, width), summary_rows(values_in, start, width)], axis=0
        )
        pieces.append([mine] + spread_z(mine))
    columns = []
    marks = []
    lines = []
    for c in range(n_chunks):
        line, mark = stack_line(pieces[c], *[cols[-1] for cols in columns[-1:]])
        shown = line
        if c + 1 < n_chunks:
            shown, _ = stack_line(pieces[c], *pieces[c + 1][1:])
        marks.append(mark)
        lines.append(shown)
        columns.append([line] + spread_columns(line))

    results = ()
    chunks = []
    cols = columns[0]
    sent, ends, after = None, [], []
    for c in range(n_chunks):
        cols = cols + [over_seq(col, 1) for col in [lines[c] if c == 0 else cols[0]] + cols[1:]]
        more = c + 1 < n_chunks
        *results, near, own, other, mark = attention(
            place, queries, keys_in, values_in, cotangent, cols, results,
            after + marks[c + 1 : c + 2], firsts[c], chunk_heads[c],
        )
        if more:
            cols = list(hold(columns[c + 1], mark))
            (other,) = hold([other], *cols)
        if sent is not None:
            *ends, mark = column_sum(sent[1])
            (other,) = hold([other], mark)
            ends = [ends[0]] + spread_z_back(ends, over_z)
            chunks.append([sent[0]] + ends)
        *sums, mark = core_sum(own, over_seq(other, 1))
        after = [mark]
        back = [over_seq(sums[i], 2 * i) for i in reversed(range(1, n_cols))][::-1]
        sent = near, [sums[0]] + back
    *ends, mark = column_sum(sent[1], *ends[1:])
    chunks.append([sent[0], ends[0]] + spread_z_back(ends, over_z))
    attended, grad_queries, dk, dv = results
    grad_keys, grad_values = finish(dk, dv, chunks)
    return (attended, grad_queries, grad_keys, grad_values)


def spread_z_back(ends, over_z):
    return [over_z(ends[j], j) for j in reversed(range(1, len(ends)))][::-1]


def solution(mesh):
    spec = P(("seq", "head"), None)
    return jax.shard_map(
        functools.partial(on_device, mesh.shape["seq"], mesh.shape["head"]),
        mesh=mesh,
        in_specs=(spec,) * 4,
        out_specs=(spec,) * 4,
        check_vma=False,
    )
```

```python
import functools
import math

import jax
import jax.numpy as jnp
from jax import lax
from jax.experimental import pallas as pl
from jax.experimental.pallas import tpu as pltpu
from jax.sharding import PartitionSpec as P

HEADS = 16
HEAD_DIM = 128
BLOCK = 128
SUMMARY = 8
EDGE = 16

neg_fill = -1e30
scaling = 1.0 / math.sqrt(HEAD_DIM)
exponent = scaling / math.log(2.0)
chunk_heads = (4, 4)
unroll = 2
vmem_bytes = 40 * 1024 * 1024
in_vmem = pl.BlockSpec(memory_space=pltpu.VMEM)
in_hbm = pl.BlockSpec(memory_space=pltpu.HBM)
in_smem = pl.BlockSpec(memory_space=pltpu.SMEM)
params = pltpu.CompilerParams(vmem_limit_bytes=vmem_bytes)


def dot(left, right, left_dim, right_dim):
    return lax.dot_general(
        left, right, (((left_dim,), (right_dim,)), ((), ())), preferred_element_type=jnp.float32
    )


def block_mask():
    key = lax.broadcasted_iota(jnp.int32, (BLOCK, BLOCK), 1)
    query = lax.broadcasted_iota(jnp.int32, (BLOCK, BLOCK), 0)
    return jnp.where(key <= query, 0.0, neg_fill)


def far_mask(seq_pos, z_pos, n_cols, nz, n_sum, tokens):
    shape = (2 * tokens, n_cols * nz * 2 * n_sum)
    key = lax.broadcasted_iota(jnp.int32, shape, 1)
    query = lax.broadcasted_iota(jnp.int32, shape, 0)
    piece = key // n_sum
    column = piece // (2 * nz)
    source = (seq_pos ^ (2 * column + piece % 2)) * nz + (z_pos ^ ((piece // 2) % nz))
    here = (seq_pos ^ (query // tokens)) * nz + z_pos
    before = (key % n_sum) // SUMMARY < (query % tokens) // BLOCK
    return jnp.where((source < here) | ((source == here) & before), 0.0, neg_fill)


def core_window(place_ref, flip, half, at, size):
    core = (place_ref[0] + flip) % 2
    return pl.ds(pl.multiple_of(core * half + at, HEAD_DIM), size)


def pack_body(place_ref, *refs):
    sources, (mine_ref, other_ref, away_ref, tiles, tile_sem, sem) = refs[:4], refs[4:]
    tokens, width = sources[0].shape
    n_blocks = tokens // BLOCK
    half = width // 2
    copies = []
    for i, source in enumerate(sources[1:3]):
        for b in range(n_blocks):
            row = i * n_blocks + b
            tile = pl.ds((b + 1) * BLOCK - EDGE, EDGE)
            copies.append(pltpu.make_async_copy(source.at[tile, :], tiles.at[row], tile_sem.at[row]))
    columns = [
        pltpu.make_async_copy(
            source.at[:, core_window(place_ref, 1, half, 0, half)], away_ref.at[i], sem.at[i]
        )
        for i, source in enumerate(sources)
    ]
    for copy in copies + columns:
        copy.start()
    for copy in copies:
        copy.wait()
    for flip, target in enumerate((mine_ref, other_ref)):
        to = core_window(place_ref, flip, half, 0, half)
        rows = [tiles[row, EDGE - SUMMARY :, to] for row in range(2 * n_blocks)]
        target[...] = jnp.concatenate(rows, axis=0)
    for copy in columns:
        copy.wait()


def pack(place, arrays):
    tokens, width = arrays[0].shape
    kind = arrays[0].dtype
    n_blocks = tokens // BLOCK
    shape = jax.ShapeDtypeStruct((2 * n_blocks * SUMMARY, width // 2), kind)
    return pl.pallas_call(
        pack_body,
        in_specs=[in_smem] + [in_hbm] * 4,
        out_specs=[in_vmem] * 3,
        out_shape=[shape] * 2 + [jax.ShapeDtypeStruct((4, tokens, width // 2), kind)],
        scratch_shapes=[
            pltpu.VMEM((2 * n_blocks, EDGE, width), kind),
            pltpu.SemaphoreType.DMA((2 * n_blocks,)),
            pltpu.SemaphoreType.DMA((4,)),
        ],
        compiler_params=params,
        name="pack",
    )(place, *[pltpu.with_memory_space_constraint(x, pltpu.HBM) for x in arrays])


def join_body(at, mine_ref, came_ref, *refs):
    ref = refs[-1]
    rows, width = mine_ref.shape[0], ref.shape[1]
    ref[:rows] = mine_ref[:, at : at + width]
    ref[rows:] = came_ref[:, at : at + width]


def join(mine, came, at, size, *after):
    return pl.pallas_call(
        functools.partial(join_body, at),
        in_specs=[in_vmem] * (2 + len(after)),
        out_specs=in_vmem,
        out_shape=jax.ShapeDtypeStruct((2 * mine.shape[0], size), mine.dtype),
        compiler_params=params,
        name="join",
    )(mine, came, *after)


def attention_body(n_sum, n_cols, n_skip, first, heads, *refs):
    place_ref = refs[0]
    sources, came_ref = refs[1:5], refs[5]
    col_refs = refs[6 : 6 + n_cols]
    outs = refs[6 + n_cols + n_skip :]
    targets = outs[:4]
    sent_ref, near_ref = outs[4:6]
    back_refs = outs[6 : 6 + n_cols]
    near_mask, away_mask, loads, stores, load_sem, store_sem = outs[6 + n_cols :]
    tokens, width = sources[0].shape
    nz = col_refs[0].shape[0]
    steps = heads // unroll
    span = unroll * HEAD_DIM

    def window(step):
        return core_window(place_ref, 0, width // 2, first * HEAD_DIM + step * span, span)

    def load(step, i):
        return pltpu.make_async_copy(
            sources[i].at[:, window(step)], loads.at[step, i], load_sem.at[step, i]
        )

    def store(step, i):
        return pltpu.make_async_copy(
            stores.at[step, i], targets[i].at[:, window(step)], store_sem.at[step, i]
        )

    for step in range(steps):
        for i in range(4):
            load(step, i).start()
    n_blocks = tokens // BLOCK
    blocks = [slice(b * BLOCK, (b + 1) * BLOCK) for b in range(2 * n_blocks)]
    near_mask[...] = block_mask()
    away_mask[...] = far_mask(place_ref[0], place_ref[1], n_cols, nz, n_sum, tokens)

    def here(to):
        return pl.ds(pl.multiple_of(first * HEAD_DIM + to.start, HEAD_DIM), HEAD_DIM)

    def far_rows(offset, to):
        parts = []
        for ref in col_refs:
            for j in range(nz):
                for core in range(2):
                    row = 2 * core * n_sum + offset
                    parts.append(ref[j, row : row + n_sum, to])
        return jnp.concatenate(parts, axis=0)

    def keep(step, i, at, to, b, value):
        if b < n_blocks:
            stores[step, i, blocks[b], at] = value
        else:
            sent_ref[i, blocks[b - n_blocks], here(to)] = value

    def head(step, at, to):
        q, k_loc, v_loc, g = (
            jnp.concatenate([loads[step, i, :, at], came_ref[i, :, here(to)]], axis=0) for i in range(4)
        )
        k_far = far_rows(0, to)
        v_far = far_rows(n_sum, to)
        mask = near_mask[...]
        s_loc = jnp.concatenate([dot(q[b], k_loc[b], 1, 1) + mask for b in blocks], axis=0)
        s_far = dot(q, k_far, 1, 1) + away_mask[...]
        high = jnp.maximum(
            jnp.max(s_loc, axis=1, keepdims=True), jnp.max(s_far, axis=1, keepdims=True)
        )
        e_loc = jnp.exp2((s_loc - high) * exponent)
        e_far = jnp.exp2((s_far - high) * exponent)
        norm = jnp.sum(e_loc, axis=1, keepdims=True) + jnp.sum(e_far, axis=1, keepdims=True)
        inv = 1.0 / norm
        eb_loc = e_loc.astype(jnp.bfloat16)
        eb_far = e_far.astype(jnp.bfloat16)
        out = jnp.concatenate([dot(eb_loc[b], v_loc[b], 1, 0) for b in blocks], axis=0) + dot(
            eb_far, v_far, 1, 0
        )
        out = (out * inv).astype(jnp.bfloat16)
        gf = g.astype(jnp.float32)
        delta = jnp.sum(gf * out.astype(jnp.float32), axis=1, keepdims=True)
        factor = inv * scaling
        t_loc = jnp.concatenate([dot(g[b], v_loc[b], 1, 1) for b in blocks], axis=0)
        t_loc = (t_loc - delta) * factor
        t_far = (dot(g, v_far, 1, 1) - delta) * factor
        ds_loc = (eb_loc.astype(jnp.float32) * t_loc).astype(jnp.bfloat16)
        ds_far = (eb_far.astype(jnp.float32) * t_far).astype(jnp.bfloat16)
        dq = jnp.concatenate([dot(ds_loc[b], k_loc[b], 1, 0) for b in blocks], axis=0) + dot(
            ds_far, k_far, 1, 0
        )
        dq = dq.astype(jnp.bfloat16)
        gi = (gf * inv).astype(jnp.bfloat16)
        for n, b in enumerate(blocks):
            keep(step, 0, at, to, n, out[b])
            keep(step, 1, at, to, n, dq[b])
            for i, (left, right) in enumerate(((ds_loc, q), (eb_loc, gi))):
                part = dot(left[b], right[b], 0, 0)
                keep(step, 2 + i, at, to, n, part.astype(jnp.bfloat16))
                t, row = n // n_blocks, (i * n_blocks + n % n_blocks) * EDGE
                near_ref[t, row : row + EDGE, to] = part[BLOCK - EDGE :, :]
        dk_far = dot(q, ds_far, 0, 0).astype(jnp.bfloat16).T
        dv_far = dot(gi, eb_far, 0, 0).astype(jnp.bfloat16).T
        row = 0
        for ref in back_refs:
            for j in range(nz):
                for core in range(2):
                    to_row = 2 * core * n_sum
                    ref[j, to_row : to_row + n_sum, to] = dk_far[row : row + n_sum]
                    ref[j, to_row + n_sum : to_row + 2 * n_sum, to] = dv_far[row : row + n_sum]
                    row += n_sum

    def turn(step, carried):
        for i in range(4):
            load(step, i).wait()
        for u in range(unroll):
            to = pl.ds(pl.multiple_of(step * span + u * HEAD_DIM, HEAD_DIM), HEAD_DIM)
            head(step, slice(u * HEAD_DIM, (u + 1) * HEAD_DIM), to)
        for i in range(4):
            store(step, i).start()
        return carried

    lax.fori_loop(0, steps, turn, 0)
    for step in range(steps):
        for i in range(4):
            store(step, i).wait()


def attention(place, mine, came, cols, earlier, after, first, heads):
    tokens, width = mine[0].shape
    n_cols = len(cols)
    nz, rows, chunk_width = cols[0].shape
    n_sum = rows // 4
    nkeys = n_cols * nz * rows // 2
    n_blocks = tokens // BLOCK
    steps = heads // unroll
    full = jax.ShapeDtypeStruct((tokens, width), jnp.bfloat16)
    n_skip = len(earlier) + len(after)
    rest = [
        jax.ShapeDtypeStruct((4, tokens, width // 2), jnp.bfloat16),
        jax.ShapeDtypeStruct((2, 2 * n_blocks * EDGE, chunk_width), jnp.float32),
    ] + [jax.ShapeDtypeStruct((nz, rows, chunk_width), jnp.bfloat16)] * n_cols
    mine = [pltpu.with_memory_space_constraint(x, pltpu.HBM) for x in mine]
    return pl.pallas_call(
        functools.partial(attention_body, n_sum, n_cols, n_skip, first, heads),
        in_specs=[in_smem]
        + [in_hbm] * 4
        + [in_vmem] * (1 + n_cols)
        + [in_hbm] * len(earlier[:4])
        + [in_vmem] * (len(earlier[4:]) + len(after)),
        out_specs=[in_hbm] * 4 + [in_vmem] * len(rest),
        out_shape=[full] * 4 + rest,
        scratch_shapes=[
            pltpu.VMEM((BLOCK, BLOCK), jnp.float32),
            pltpu.VMEM((2 * tokens, nkeys), jnp.float32),
            pltpu.VMEM((steps, 4, tokens, unroll * HEAD_DIM), jnp.bfloat16),
            pltpu.VMEM((steps, 4, tokens, unroll * HEAD_DIM), jnp.bfloat16),
            pltpu.SemaphoreType.DMA((steps, 4)),
            pltpu.SemaphoreType.DMA((steps, 4)),
        ],
        input_output_aliases={6 + n_cols + i: i for i in range(len(earlier))},
        compiler_params=params,
        cost_estimate=pl.CostEstimate(
            flops=heads * 24 * tokens * (BLOCK + nkeys) * HEAD_DIM,
            bytes_accessed=heads * HEAD_DIM * (32 * tokens + 8 * nkeys),
            transcendentals=heads * 2 * tokens * (BLOCK + nkeys),
        ),
        name="attention",
    )(place, *mine, came, *cols, *earlier, *after)


def hold_body(*refs):
    pass


def hold(arrays, *after):
    return pl.pallas_call(
        hold_body,
        in_specs=[in_vmem] * (len(arrays) + len(after)),
        out_specs=[in_vmem] * len(arrays),
        out_shape=[jax.ShapeDtypeStruct(a.shape, a.dtype) for a in arrays],
        input_output_aliases={i: i for i in range(len(arrays))},
        compiler_params=params,
        name="hold",
    )(*arrays, *after)


def line_body(n_in, *refs):
    for j in range(n_in):
        refs[-1][j] = refs[j][...]


def stack_line(pieces, *after):
    return pl.pallas_call(
        functools.partial(line_body, len(pieces)),
        in_specs=[in_vmem] * (len(pieces) + len(after)),
        out_specs=in_vmem,
        out_shape=jax.ShapeDtypeStruct((len(pieces),) + pieces[0].shape, pieces[0].dtype),
        compiler_params=params,
        name="line",
    )(*pieces, *after)


def column_sum_body(n_in, n_after, *refs):
    in_refs, out_refs = refs[:n_in], refs[n_in + n_after :]
    for j, ref in enumerate(out_refs):
        total = in_refs[0][j].astype(jnp.float32)
        for came in in_refs[1:]:
            total = total + came[j].astype(jnp.float32)
        ref[...] = total.astype(ref.dtype)


def column_sum(parts, *after):
    nz = parts[0].shape[0]
    shapes = [
        jax.ShapeDtypeStruct(parts[0].shape[1:], jnp.float32 if j == 0 else jnp.bfloat16)
        for j in range(nz)
    ]
    return pl.pallas_call(
        functools.partial(column_sum_body, len(parts), len(after)),
        in_specs=[in_vmem] * (len(parts) + len(after)),
        out_specs=[in_vmem] * nz,
        out_shape=shapes,
        compiler_params=params,
        name="column_sum",
    )(*parts, *after)


def edge_body(n_terms, *refs):
    terms, targets = refs[:-2], refs[-2:]
    at = 0
    for c in range(0, len(terms), n_terms):
        near_ref, *ends = terms[c : c + n_terms]
        total = ends[0][...]
        for term in ends[1:]:
            total = total + term[...].astype(jnp.float32)
        rows = total.shape[0] // 2
        to = slice(at, at + total.shape[1])
        at += total.shape[1]
        for t, target in enumerate(targets):
            for n in range(rows // SUMMARY):
                tile = near_ref[t, n * EDGE : (n + 1) * EDGE, :]
                more = total[t * rows + n * SUMMARY : t * rows + (n + 1) * SUMMARY]
                tile = [tile[: EDGE - SUMMARY], tile[EDGE - SUMMARY :] + more]
                tile = jnp.concatenate(tile, axis=0).astype(target.dtype)
                target[n * EDGE : (n + 1) * EDGE, to] = tile


def edge(chunks):
    width = sum(chunk[0].shape[2] for chunk in chunks)
    shape = jax.ShapeDtypeStruct((chunks[0][0].shape[1], width), jnp.bfloat16)
    return pl.pallas_call(
        functools.partial(edge_body, len(chunks[0])),
        in_specs=[in_vmem] * (len(chunks) * len(chunks[0])),
        out_specs=[in_vmem] * 2,
        out_shape=[shape] * 2,
        compiler_params=params,
        name="edge",
    )(*[term for chunk in chunks for term in chunk])


def settle_body(n_came, place_ref, *refs):
    came_refs, targets = refs[:n_came], refs[n_came + 4 : n_came + 8]
    sem = refs[n_came + 8]
    width = targets[0].shape[1]
    copies = []
    at = 0
    for c, came in enumerate(came_refs):
        to = core_window(place_ref, 1, width // 2, at, came.shape[2])
        at += came.shape[2]
        for i, target in enumerate(targets):
            copies.append(pltpu.make_async_copy(came.at[i], target.at[:, to], sem.at[c, i]))
    for copy in copies:
        copy.start()
    for copy in copies:
        copy.wait()


def settle(place, came, results):
    n = len(came)
    return pl.pallas_call(
        functools.partial(settle_body, n),
        in_specs=[in_smem] + [in_vmem] * n + [in_hbm] * 4,
        out_specs=[in_hbm] * 4,
        out_shape=[jax.ShapeDtypeStruct(x.shape, x.dtype) for x in results],
        scratch_shapes=[pltpu.SemaphoreType.DMA((n, 4))],
        input_output_aliases={1 + n + i: i for i in range(4)},
        compiler_params=params,
        name="settle",
    )(place, *came, *results)


def finish_body(n_edges, n_blocks, place_ref, *refs):
    edges = refs[2 : 2 + n_edges]
    targets, sem = refs[2 + n_edges : 4 + n_edges], refs[4 + n_edges]
    width = targets[0].shape[1]
    copies = []
    at = 0
    for e, source in enumerate(edges):
        flip = e % 2
        to = core_window(place_ref, flip, width // 2, at, source.shape[1])
        at += flip * source.shape[1]
        for n in range(2 * n_blocks):
            i, b = divmod(n, n_blocks)
            copies.append(
                pltpu.make_async_copy(
                    source.at[pl.ds(n * EDGE, EDGE)],
                    targets[i].at[pl.ds((b + 1) * BLOCK - EDGE, EDGE), to],
                    sem.at[e, n],
                )
            )
    for copy in copies:
        copy.start()
    for copy in copies:
        copy.wait()


def finish(place, dk, dv, edges):
    n_blocks = dk.shape[0] // BLOCK
    return pl.pallas_call(
        functools.partial(finish_body, len(edges), n_blocks),
        in_specs=[in_smem] + [in_hbm] * 2 + [in_vmem] * len(edges),
        out_specs=[in_hbm] * 2,
        out_shape=[jax.ShapeDtypeStruct(dk.shape, dk.dtype)] * 2,
        scratch_shapes=[pltpu.SemaphoreType.DMA((len(edges), 2 * n_blocks))],
        input_output_aliases={1: 0, 2: 1},
        compiler_params=params,
        name="finish",
    )(place, dk, dv, *edges)


def on_device(n_seq, nz, queries, keys_in, values_in, cotangent):
    n_cols = n_seq // 2
    n_chunks = len(chunk_heads)
    firsts = [sum(chunk_heads[:c]) for c in range(n_chunks)]

    def over_z(array, bits):
        return lax.ppermute(array, "head", [(i, i ^ bits) for i in range(nz)])

    def over_seq(array, bits):
        return lax.ppermute(array, "seq", [(i, i ^ bits) for i in range(n_seq)])

    def swap_z(pieces):
        return [over_z(pieces[j], j) for j in reversed(range(1, nz))][::-1]

    def swap_columns(parts):
        return [over_seq(parts[c], 2 * c) for c in reversed(range(1, n_cols))][::-1]

    place = jnp.stack([lax.axis_index("seq"), lax.axis_index("head")]).astype(jnp.int32)
    arrays = (queries, keys_in, values_in, cotangent)
    mine, other, part = pack(place, arrays)
    came = over_seq(other, 1)
    columns = []
    theirs = None
    for c in range(n_chunks):
        width = chunk_heads[c] * HEAD_DIM
        start = join(mine, came, firsts[c] * HEAD_DIM, width, *([theirs] if c else []))
        pieces = [start] + swap_z([start] * nz)
        if c == 0:
            theirs = over_seq(hold([part], *pieces[1:])[0], 1)
        line = stack_line(pieces, *[cols[-1] for cols in columns[-1:]])
        columns.append([line] + swap_columns([line] * n_cols))

    results = ()
    chunks = []
    back = None
    for c in range(n_chunks):
        made = attention(
            place,
            arrays,
            theirs,
            columns[c],
            results,
            [cols[0] for cols in columns[c + 1 : c + 2]],
            firsts[c],
            chunk_heads[c],
        )
        results, near, parts = made[:5], made[5], list(made[6:])
        waits = columns[c + 1][1:] if c + 1 < n_chunks else []
        if back is not None:
            ends = column_sum(back[1], near)
            waits = waits + list(ends[:1])
        moved = swap_columns(parts[:1] + list(hold(parts[1:], *waits)))
        if back is not None:
            chunks.append([back[0], ends[0]] + swap_z(ends))
        back = near, parts[:1] + moved
    ends = column_sum(back[1], *chunks[-1][2:])
    chunks.append([back[0], ends[0]] + swap_z(ends))
    *results, sent = results
    (sent,) = hold([sent], ends[0])
    results = settle(place, [over_seq(sent, 1)], results)
    own, away = edge(chunks)
    attended, grad_queries, dk, dv = results
    edges = [own, over_seq(away, 1)]
    grad_keys, grad_values = finish(place, dk, dv, edges)
    return (attended, grad_queries, grad_keys, grad_values)


def solution(mesh):
    spec = P(("seq", "head"), None)
    return jax.shard_map(
        functools.partial(on_device, mesh.shape["seq"], mesh.shape["head"]),
        mesh=mesh,
        in_specs=(spec,) * 4,
        out_specs=(spec,) * 4,
        check_vma=False,
    )
```

```python
import functools
import math

import jax
import jax.numpy as jnp
from jax import lax
from jax.experimental import pallas as pl
from jax.experimental.pallas import tpu as pltpu
from jax.sharding import PartitionSpec as P

HEADS = 16
HEAD_DIM = 128
BLOCK = 128
SUMMARY = 8
EDGE = 16

neg_fill = -1e30
scaling = 1.0 / math.sqrt(HEAD_DIM)
exponent = scaling / math.log(2.0)
chunk_heads = (4, 4)
unroll = 2
vmem_bytes = 40 * 1024 * 1024
in_vmem = pl.BlockSpec(memory_space=pltpu.VMEM)
in_hbm = pl.BlockSpec(memory_space=pltpu.HBM)
in_smem = pl.BlockSpec(memory_space=pltpu.SMEM)
params = pltpu.CompilerParams(vmem_limit_bytes=vmem_bytes)


def dot(left, right, left_dim, right_dim):
    return lax.dot_general(
        left, right, (((left_dim,), (right_dim,)), ((), ())), preferred_element_type=jnp.float32
    )


def block_mask():
    key = lax.broadcasted_iota(jnp.int32, (BLOCK, BLOCK), 1)
    query = lax.broadcasted_iota(jnp.int32, (BLOCK, BLOCK), 0)
    return jnp.where(key <= query, 0.0, neg_fill)


def far_mask(seq_pos, z_pos, n_cols, nz, n_sum, tokens):
    shape = (2 * tokens, n_cols * nz * 2 * n_sum)
    key = lax.broadcasted_iota(jnp.int32, shape, 1)
    query = lax.broadcasted_iota(jnp.int32, shape, 0)
    piece = key // n_sum
    column = piece // (2 * nz)
    source = (seq_pos ^ (2 * column + piece % 2)) * nz + (z_pos ^ ((piece // 2) % nz))
    here = (seq_pos ^ (query // tokens)) * nz + z_pos
    before = (key % n_sum) // SUMMARY < (query % tokens) // BLOCK
    return jnp.where((source < here) | ((source == here) & before), 0.0, neg_fill)


def core_window(place_ref, flip, half, at, size):
    core = (place_ref[0] + flip) % 2
    return pl.ds(pl.multiple_of(core * half + at, HEAD_DIM), size)


def pack_body(place_ref, *refs):
    sources, (mine_ref, other_ref, away_ref, tiles, tile_sem, sem) = refs[:4], refs[4:]
    tokens, width = sources[0].shape
    n_blocks = tokens // BLOCK
    half = width // 2
    copies = []
    for i, source in enumerate(sources[1:3]):
        for b in range(n_blocks):
            row = i * n_blocks + b
            tile = pl.ds((b + 1) * BLOCK - EDGE, EDGE)
            copies.append(pltpu.make_async_copy(source.at[tile, :], tiles.at[row], tile_sem.at[row]))
    columns = [
        pltpu.make_async_copy(
            source.at[:, core_window(place_ref, 1, half, 0, half)], away_ref.at[i], sem.at[i]
        )
        for i, source in enumerate(sources)
    ]
    for copy in copies + columns:
        copy.start()
    for copy in copies:
        copy.wait()
    for flip, target in enumerate((mine_ref, other_ref)):
        to = core_window(place_ref, flip, half, 0, half)
        rows = [tiles[row, EDGE - SUMMARY :, to] for row in range(2 * n_blocks)]
        target[...] = jnp.concatenate(rows, axis=0)
    for copy in columns:
        copy.wait()


def pack(place, arrays):
    tokens, width = arrays[0].shape
    kind = arrays[0].dtype
    n_blocks = tokens // BLOCK
    shape = jax.ShapeDtypeStruct((2 * n_blocks * SUMMARY, width // 2), kind)
    return pl.pallas_call(
        pack_body,
        in_specs=[in_smem] + [in_hbm] * 4,
        out_specs=[in_vmem] * 3,
        out_shape=[shape] * 2 + [jax.ShapeDtypeStruct((4, tokens, width // 2), kind)],
        scratch_shapes=[
            pltpu.VMEM((2 * n_blocks, EDGE, width), kind),
            pltpu.SemaphoreType.DMA((2 * n_blocks,)),
            pltpu.SemaphoreType.DMA((4,)),
        ],
        compiler_params=params,
        name="pack",
    )(place, *[pltpu.with_memory_space_constraint(x, pltpu.HBM) for x in arrays])


def join_body(at, mine_ref, came_ref, *refs):
    ref = refs[-1]
    rows, width = mine_ref.shape[0], ref.shape[1]
    ref[:rows] = mine_ref[:, at : at + width]
    ref[rows:] = came_ref[:, at : at + width]


def join(mine, came, at, size, *after):
    return pl.pallas_call(
        functools.partial(join_body, at),
        in_specs=[in_vmem] * (2 + len(after)),
        out_specs=in_vmem,
        out_shape=jax.ShapeDtypeStruct((2 * mine.shape[0], size), mine.dtype),
        compiler_params=params,
        name="join",
    )(mine, came, *after)


def attention_body(n_sum, n_cols, n_skip, first, heads, *refs):
    place_ref = refs[0]
    sources, came_ref = refs[1:5], refs[5]
    col_refs = refs[6 : 6 + n_cols]
    outs = refs[6 + n_cols + n_skip :]
    targets = outs[:4]
    sent_ref, near_ref = outs[4:6]
    back_refs = outs[6 : 6 + n_cols]
    near_mask, away_mask, loads, stores, load_sem, store_sem = outs[6 + n_cols :]
    tokens, width = sources[0].shape
    nz = col_refs[0].shape[0]
    steps = heads // unroll
    span = unroll * HEAD_DIM

    def window(step):
        return core_window(place_ref, 0, width // 2, first * HEAD_DIM + step * span, span)

    def load(step, i):
        return pltpu.make_async_copy(
            sources[i].at[:, window(step)], loads.at[step, i], load_sem.at[step, i]
        )

    def store(step, i):
        return pltpu.make_async_copy(
            stores.at[step, i], targets[i].at[:, window(step)], store_sem.at[step, i]
        )

    for step in range(steps):
        for i in range(4):
            load(step, i).start()
    n_blocks = tokens // BLOCK
    blocks = [slice(b * BLOCK, (b + 1) * BLOCK) for b in range(2 * n_blocks)]
    near_mask[...] = block_mask()
    away_mask[...] = far_mask(place_ref[0], place_ref[1], n_cols, nz, n_sum, tokens)

    def here(to):
        return pl.ds(pl.multiple_of(first * HEAD_DIM + to.start, HEAD_DIM), HEAD_DIM)

    def far_rows(offset, to):
        parts = []
        for ref in col_refs:
            for j in range(nz):
                for core in range(2):
                    row = 2 * core * n_sum + offset
                    parts.append(ref[j, row : row + n_sum, to])
        return jnp.concatenate(parts, axis=0)

    def keep(step, i, at, to, b, value):
        if b < n_blocks:
            stores[step, i, blocks[b], at] = value
        else:
            sent_ref[i, blocks[b - n_blocks], here(to)] = value

    def head(step, at, to):
        q, k_loc, v_loc, g = (
            jnp.concatenate([loads[step, i, :, at], came_ref[i, :, here(to)]], axis=0) for i in range(4)
        )
        k_far = far_rows(0, to)
        v_far = far_rows(n_sum, to)
        mask = near_mask[...]
        s_loc = jnp.concatenate([dot(q[b], k_loc[b], 1, 1) + mask for b in blocks], axis=0)
        s_far = dot(q, k_far, 1, 1) + away_mask[...]
        high = jnp.maximum(
            jnp.max(s_loc, axis=1, keepdims=True), jnp.max(s_far, axis=1, keepdims=True)
        )
        e_loc = jnp.exp2((s_loc - high) * exponent)
        e_far = jnp.exp2((s_far - high) * exponent)
        norm = jnp.sum(e_loc, axis=1, keepdims=True) + jnp.sum(e_far, axis=1, keepdims=True)
        inv = 1.0 / norm
        eb_loc = e_loc.astype(jnp.bfloat16)
        eb_far = e_far.astype(jnp.bfloat16)
        out = jnp.concatenate([dot(eb_loc[b], v_loc[b], 1, 0) for b in blocks], axis=0) + dot(
            eb_far, v_far, 1, 0
        )
        out = (out * inv).astype(jnp.bfloat16)
        gf = g.astype(jnp.float32)
        delta = jnp.sum(gf * out.astype(jnp.float32), axis=1, keepdims=True)
        factor = inv * scaling
        t_loc = jnp.concatenate([dot(g[b], v_loc[b], 1, 1) for b in blocks], axis=0)
        t_loc = (t_loc - delta) * factor
        t_far = (dot(g, v_far, 1, 1) - delta) * factor
        ds_loc = (eb_loc.astype(jnp.float32) * t_loc).astype(jnp.bfloat16)
        ds_far = (eb_far.astype(jnp.float32) * t_far).astype(jnp.bfloat16)
        dq = jnp.concatenate([dot(ds_loc[b], k_loc[b], 1, 0) for b in blocks], axis=0) + dot(
            ds_far, k_far, 1, 0
        )
        dq = dq.astype(jnp.bfloat16)
        gi = (gf * inv).astype(jnp.bfloat16)
        for n, b in enumerate(blocks):
            keep(step, 0, at, to, n, out[b])
            keep(step, 1, at, to, n, dq[b])
            for i, (left, right) in enumerate(((ds_loc, q), (eb_loc, gi))):
                part = dot(left[b], right[b], 0, 0)
                keep(step, 2 + i, at, to, n, part.astype(jnp.bfloat16))
                t, row = n // n_blocks, (i * n_blocks + n % n_blocks) * EDGE
                near_ref[t, row : row + EDGE, to] = part[BLOCK - EDGE :, :]
        dk_far = dot(q, ds_far, 0, 0).astype(jnp.bfloat16).T
        dv_far = dot(gi, eb_far, 0, 0).astype(jnp.bfloat16).T
        row = 0
        for ref in back_refs:
            for j in range(nz):
                for core in range(2):
                    to_row = 2 * core * n_sum
                    ref[j, to_row : to_row + n_sum, to] = dk_far[row : row + n_sum]
                    ref[j, to_row + n_sum : to_row + 2 * n_sum, to] = dv_far[row : row + n_sum]
                    row += n_sum

    def turn(step, carried):
        for i in range(4):
            load(step, i).wait()
        for u in range(unroll):
            to = pl.ds(pl.multiple_of(step * span + u * HEAD_DIM, HEAD_DIM), HEAD_DIM)
            head(step, slice(u * HEAD_DIM, (u + 1) * HEAD_DIM), to)
        for i in range(4):
            store(step, i).start()
        return carried

    lax.fori_loop(0, steps, turn, 0)
    for step in range(steps):
        for i in range(4):
            store(step, i).wait()


def attention(place, mine, came, cols, earlier, after, first, heads):
    tokens, width = mine[0].shape
    n_cols = len(cols)
    nz, rows, chunk_width = cols[0].shape
    n_sum = rows // 4
    nkeys = n_cols * nz * rows // 2
    n_blocks = tokens // BLOCK
    steps = heads // unroll
    full = jax.ShapeDtypeStruct((tokens, width), jnp.bfloat16)
    n_skip = len(earlier) + len(after)
    rest = [
        jax.ShapeDtypeStruct((4, tokens, width // 2), jnp.bfloat16),
        jax.ShapeDtypeStruct((2, 2 * n_blocks * EDGE, chunk_width), jnp.float32),
    ] + [jax.ShapeDtypeStruct((nz, rows, chunk_width), jnp.bfloat16)] * n_cols
    mine = [pltpu.with_memory_space_constraint(x, pltpu.HBM) for x in mine]
    return pl.pallas_call(
        functools.partial(attention_body, n_sum, n_cols, n_skip, first, heads),
        in_specs=[in_smem]
        + [in_hbm] * 4
        + [in_vmem] * (1 + n_cols)
        + [in_hbm] * len(earlier[:4])
        + [in_vmem] * (len(earlier[4:]) + len(after)),
        out_specs=[in_hbm] * 4 + [in_vmem] * len(rest),
        out_shape=[full] * 4 + rest,
        scratch_shapes=[
            pltpu.VMEM((BLOCK, BLOCK), jnp.float32),
            pltpu.VMEM((2 * tokens, nkeys), jnp.float32),
            pltpu.VMEM((steps, 4, tokens, unroll * HEAD_DIM), jnp.bfloat16),
            pltpu.VMEM((steps, 4, tokens, unroll * HEAD_DIM), jnp.bfloat16),
            pltpu.SemaphoreType.DMA((steps, 4)),
            pltpu.SemaphoreType.DMA((steps, 4)),
        ],
        input_output_aliases={6 + n_cols + i: i for i in range(len(earlier))},
        compiler_params=params,
        cost_estimate=pl.CostEstimate(
            flops=heads * 24 * tokens * (BLOCK + nkeys) * HEAD_DIM,
            bytes_accessed=heads * HEAD_DIM * (32 * tokens + 8 * nkeys),
            transcendentals=heads * 2 * tokens * (BLOCK + nkeys),
        ),
        name="attention",
    )(place, *mine, came, *cols, *earlier, *after)


def hold_body(*refs):
    pass


def hold(arrays, *after):
    return pl.pallas_call(
        hold_body,
        in_specs=[in_vmem] * (len(arrays) + len(after)),
        out_specs=[in_vmem] * len(arrays),
        out_shape=[jax.ShapeDtypeStruct(a.shape, a.dtype) for a in arrays],
        input_output_aliases={i: i for i in range(len(arrays))},
        compiler_params=params,
        name="hold",
    )(*arrays, *after)


def line_body(at, n_far, own_ref, pair_ref, *refs):
    line_ref = refs[-1]
    line_ref[0] = own_ref[...]
    line_ref[1] = pair_ref[:, at : at + own_ref.shape[1]]
    for j in range(n_far):
        line_ref[2 + j] = refs[j][...]


def stack_line(own, pair, far, at, *after):
    return pl.pallas_call(
        functools.partial(line_body, at, len(far)),
        in_specs=[in_vmem] * (2 + len(far) + len(after)),
        out_specs=in_vmem,
        out_shape=jax.ShapeDtypeStruct((2 + len(far),) + own.shape, own.dtype),
        compiler_params=params,
        name="line",
    )(own, pair, *far, *after)


def column_sum_body(n_in, n_pairs, n_after, *refs):
    in_refs, pair_refs = refs[:n_in], refs[n_in : n_in + n_pairs]
    out_refs = refs[n_in + n_pairs + n_after :]
    for j, ref in enumerate(out_refs):
        total = in_refs[0][j].astype(jnp.float32)
        for came in in_refs[1:]:
            total = total + came[j].astype(jnp.float32)
        at = 0
        if j == 1:
            for pair in pair_refs:
                ref[:, at : at + pair.shape[1]] = pair[...]
                at += pair.shape[1]
        ref[:, at : at + total.shape[1]] = total.astype(ref.dtype)


def column_sum(parts, pairs, *after):
    nz, rows, width = parts[0].shape
    shapes = [
        jax.ShapeDtypeStruct((rows, width), jnp.float32 if j == 0 else jnp.bfloat16)
        for j in range(nz)
    ]
    wide = width + sum(pair.shape[1] for pair in pairs)
    shapes[1] = jax.ShapeDtypeStruct((rows, wide), jnp.bfloat16)
    return pl.pallas_call(
        functools.partial(column_sum_body, len(parts), len(pairs), len(after)),
        in_specs=[in_vmem] * (len(parts) + len(pairs) + len(after)),
        out_specs=[in_vmem] * nz,
        out_shape=shapes,
        compiler_params=params,
        name="column_sum",
    )(*parts, *pairs, *after)


def edge_body(n_chunks, n_terms, pair_ref, *refs):
    terms, targets = refs[: n_chunks * n_terms], refs[-2:]
    at = 0
    for c in range(0, len(terms), n_terms):
        near_ref, *ends = terms[c : c + n_terms]
        to = slice(at, at + near_ref.shape[2])
        at += near_ref.shape[2]
        total = ends[0][...] + pair_ref[:, to].astype(jnp.float32)
        for term in ends[1:]:
            total = total + term[...].astype(jnp.float32)
        rows = total.shape[0] // 2
        for t, target in enumerate(targets):
            for n in range(rows // SUMMARY):
                tile = near_ref[t, n * EDGE : (n + 1) * EDGE, :]
                more = total[t * rows + n * SUMMARY : t * rows + (n + 1) * SUMMARY]
                tile = [tile[: EDGE - SUMMARY], tile[EDGE - SUMMARY :] + more]
                tile = jnp.concatenate(tile, axis=0).astype(target.dtype)
                target[n * EDGE : (n + 1) * EDGE, to] = tile


def edge(pair, chunks, *after):
    width = sum(chunk[0].shape[2] for chunk in chunks)
    shape = jax.ShapeDtypeStruct((chunks[0][0].shape[1], width), jnp.bfloat16)
    terms = [term for chunk in chunks for term in chunk]
    return pl.pallas_call(
        functools.partial(edge_body, len(chunks), len(chunks[0])),
        in_specs=[in_vmem] * (1 + len(terms) + len(after)),
        out_specs=[in_vmem] * 2,
        out_shape=[shape] * 2,
        compiler_params=params,
        name="edge",
    )(pair, *terms, *after)


def settle_body(n_came, place_ref, *refs):
    came_refs, targets = refs[:n_came], refs[n_came + 4 : n_came + 8]
    token_ref, sem = refs[n_came + 8 :]
    token_ref[...] = jnp.zeros(token_ref.shape, token_ref.dtype)
    width = targets[0].shape[1]
    copies = []
    at = 0
    for c, came in enumerate(came_refs):
        to = core_window(place_ref, 1, width // 2, at, came.shape[2])
        at += came.shape[2]
        for i, target in enumerate(targets):
            copies.append(pltpu.make_async_copy(came.at[i], target.at[:, to], sem.at[c, i]))
    for copy in copies:
        copy.start()
    for copy in copies:
        copy.wait()


def settle(place, came, results):
    n = len(came)
    return pl.pallas_call(
        functools.partial(settle_body, n),
        in_specs=[in_smem] + [in_vmem] * n + [in_hbm] * 4,
        out_specs=[in_hbm] * 4 + [in_vmem],
        out_shape=[jax.ShapeDtypeStruct(x.shape, x.dtype) for x in results]
        + [jax.ShapeDtypeStruct((8, 128), jnp.float32)],
        scratch_shapes=[pltpu.SemaphoreType.DMA((n, 4))],
        input_output_aliases={1 + n + i: i for i in range(4)},
        compiler_params=params,
        name="settle",
    )(place, *came, *results)


def finish_body(n_edges, n_blocks, place_ref, *refs):
    edges = refs[2 : 2 + n_edges]
    targets, sem = refs[2 + n_edges : 4 + n_edges], refs[4 + n_edges]
    width = targets[0].shape[1]
    copies = []
    at = 0
    for e, source in enumerate(edges):
        flip = e % 2
        to = core_window(place_ref, flip, width // 2, at, source.shape[1])
        at += flip * source.shape[1]
        for n in range(2 * n_blocks):
            i, b = divmod(n, n_blocks)
            copies.append(
                pltpu.make_async_copy(
                    source.at[pl.ds(n * EDGE, EDGE)],
                    targets[i].at[pl.ds((b + 1) * BLOCK - EDGE, EDGE), to],
                    sem.at[e, n],
                )
            )
    for copy in copies:
        copy.start()
    for copy in copies:
        copy.wait()


def finish(place, dk, dv, edges):
    n_blocks = dk.shape[0] // BLOCK
    return pl.pallas_call(
        functools.partial(finish_body, len(edges), n_blocks),
        in_specs=[in_smem] + [in_hbm] * 2 + [in_vmem] * len(edges),
        out_specs=[in_hbm] * 2,
        out_shape=[jax.ShapeDtypeStruct(dk.shape, dk.dtype)] * 2,
        scratch_shapes=[pltpu.SemaphoreType.DMA((len(edges), 2 * n_blocks))],
        input_output_aliases={1: 0, 2: 1},
        compiler_params=params,
        name="finish",
    )(place, dk, dv, *edges)


def on_device(n_seq, nz, queries, keys_in, values_in, cotangent):
    n_cols = n_seq // 2
    n_chunks = len(chunk_heads)
    firsts = [sum(chunk_heads[:c]) for c in range(n_chunks)]

    def over_z(array, bits):
        return lax.ppermute(array, "head", [(i, i ^ bits) for i in range(nz)])

    def over_seq(array, bits):
        return lax.ppermute(array, "seq", [(i, i ^ bits) for i in range(n_seq)])

    def swap_far(pieces):
        return [over_z(pieces[j], j) for j in reversed(range(2, nz))][::-1]

    def swap_columns(parts):
        return [over_seq(parts[c], 2 * c) for c in reversed(range(1, n_cols))][::-1]

    place = jnp.stack([lax.axis_index("seq"), lax.axis_index("head")]).astype(jnp.int32)
    arrays = (queries, keys_in, values_in, cotangent)
    mine, other, part = pack(place, arrays)
    came = over_seq(other, 1)
    pair = over_z(join(mine, came, 0, mine.shape[1]), 1)
    columns = []
    theirs = over_seq(hold([part], came)[0], 1)
    for c in range(n_chunks):
        width = chunk_heads[c] * HEAD_DIM
        at = firsts[c] * HEAD_DIM
        own = join(mine, came, at, width, *[cols[0] for cols in columns[-1:]])
        far = swap_far([own] * nz)
        line = stack_line(own, pair, far, at, *([cols[-1] for cols in columns[-1:]] or [theirs]))
        columns.append([line] + swap_columns([line] * n_cols))

    results = ()
    chunks, pairs = [], []
    back = None
    for c in range(n_chunks):
        made = attention(
            place,
            arrays,
            theirs,
            columns[c],
            results,
            [cols[0] for cols in columns[c + 1 : c + 2]],
            firsts[c],
            chunk_heads[c],
        )
        results, near, parts = made[:5], made[5], list(made[6:])
        waits = columns[c + 1] if c + 1 < n_chunks else [None] * n_cols
        if back is not None:
            waits = back[1]
        moved = [hold([parts[i]], waits[i])[0] for i in range(1, n_cols)]
        moved = swap_columns(parts[:1] + moved)
        if back is not None:
            ends = column_sum(back[1], [], near)
            pairs.append(ends[1])
            chunks.append([back[0], ends[0]] + swap_far(ends))
        back = near, parts[:1] + moved
    ends = column_sum(back[1], pairs, *chunks[-1][2:])
    pair = over_z(ends[1], 1)
    chunks.append([back[0], ends[0]] + swap_far(ends))
    *results, sent = results
    (sent,) = hold([sent], ends[0])
    *results, mark = settle(place, [over_seq(sent, 1)], results)
    own, away = edge(pair, chunks, mark)
    attended, grad_queries, dk, dv = results
    edges = [own, over_seq(away, 1)]
    grad_keys, grad_values = finish(place, dk, dv, edges)
    return (attended, grad_queries, grad_keys, grad_values)


def solution(mesh):
    spec = P(("seq", "head"), None)
    return jax.shard_map(
        functools.partial(on_device, mesh.shape["seq"], mesh.shape["head"]),
        mesh=mesh,
        in_specs=(spec,) * 4,
        out_specs=(spec,) * 4,
        check_vma=False,
    )
```

```python
import functools
import math

import jax
import jax.numpy as jnp
from jax import lax
from jax.experimental import pallas as pl
from jax.experimental.pallas import tpu as pltpu
from jax.sharding import PartitionSpec as P

HEADS = 16
HEAD_DIM = 128
BLOCK = 128
SUMMARY = 8
EDGE = 16

neg_fill = -1e30
scaling = 1.0 / math.sqrt(HEAD_DIM)
exponent = scaling / math.log(2.0)
chunk_heads = (4, 4)
unroll = 2
vmem_bytes = 40 * 1024 * 1024
in_vmem = pl.BlockSpec(memory_space=pltpu.VMEM)
in_hbm = pl.BlockSpec(memory_space=pltpu.HBM)
in_smem = pl.BlockSpec(memory_space=pltpu.SMEM)
params = pltpu.CompilerParams(vmem_limit_bytes=vmem_bytes)


def dot(left, right, left_dim, right_dim):
    return lax.dot_general(
        left, right, (((left_dim,), (right_dim,)), ((), ())), preferred_element_type=jnp.float32
    )


def block_mask():
    key = lax.broadcasted_iota(jnp.int32, (BLOCK, BLOCK), 1)
    query = lax.broadcasted_iota(jnp.int32, (BLOCK, BLOCK), 0)
    return jnp.where(key <= query, 0.0, neg_fill)


def far_mask(seq_pos, z_pos, n_cols, nz, n_sum, tokens):
    shape = (2 * tokens, n_cols * nz * 2 * n_sum)
    key = lax.broadcasted_iota(jnp.int32, shape, 1)
    query = lax.broadcasted_iota(jnp.int32, shape, 0)
    piece = key // n_sum
    column = piece // (2 * nz)
    source = (seq_pos ^ (2 * column + piece % 2)) * nz + (z_pos ^ ((piece // 2) % nz))
    here = (seq_pos ^ (query // tokens)) * nz + z_pos
    before = (key % n_sum) // SUMMARY < (query % tokens) // BLOCK
    return jnp.where((source < here) | ((source == here) & before), 0.0, neg_fill)


def core_window(place_ref, flip, half, at, size):
    core = (place_ref[0] + flip) % 2
    return pl.ds(pl.multiple_of(core * half + at, HEAD_DIM), size)


def pack_body(place_ref, *refs):
    sources, (mine_ref, other_ref, away_ref, tiles, tile_sem, sem) = refs[:4], refs[4:]
    tokens, width = sources[0].shape
    n_blocks = tokens // BLOCK
    half = width // 2
    copies = []
    for i, source in enumerate(sources[1:3]):
        for b in range(n_blocks):
            row = i * n_blocks + b
            tile = pl.ds((b + 1) * BLOCK - EDGE, EDGE)
            copies.append(pltpu.make_async_copy(source.at[tile, :], tiles.at[row], tile_sem.at[row]))
    columns = [
        pltpu.make_async_copy(
            source.at[:, core_window(place_ref, 1, half, 0, half)], away_ref.at[i], sem.at[i]
        )
        for i, source in enumerate(sources)
    ]
    for copy in copies + columns:
        copy.start()
    for copy in copies:
        copy.wait()
    for flip, target in enumerate((mine_ref, other_ref)):
        to = core_window(place_ref, flip, half, 0, half)
        rows = [tiles[row, EDGE - SUMMARY :, to] for row in range(2 * n_blocks)]
        target[...] = jnp.concatenate(rows, axis=0)
    for copy in columns:
        copy.wait()


def pack(place, arrays):
    tokens, width = arrays[0].shape
    kind = arrays[0].dtype
    n_blocks = tokens // BLOCK
    shape = jax.ShapeDtypeStruct((2 * n_blocks * SUMMARY, width // 2), kind)
    return pl.pallas_call(
        pack_body,
        in_specs=[in_smem] + [in_hbm] * 4,
        out_specs=[in_vmem] * 3,
        out_shape=[shape] * 2 + [jax.ShapeDtypeStruct((4, tokens, width // 2), kind)],
        scratch_shapes=[
            pltpu.VMEM((2 * n_blocks, EDGE, width), kind),
            pltpu.SemaphoreType.DMA((2 * n_blocks,)),
            pltpu.SemaphoreType.DMA((4,)),
        ],
        compiler_params=params,
        name="pack",
    )(place, *[pltpu.with_memory_space_constraint(x, pltpu.HBM) for x in arrays])


def join_body(at, mine_ref, came_ref, *refs):
    ref = refs[-1]
    rows, width = mine_ref.shape[0], ref.shape[1]
    ref[:rows] = mine_ref[:, at : at + width]
    ref[rows:] = came_ref[:, at : at + width]


def join(mine, came, at, size, *after):
    return pl.pallas_call(
        functools.partial(join_body, at),
        in_specs=[in_vmem] * (2 + len(after)),
        out_specs=in_vmem,
        out_shape=jax.ShapeDtypeStruct((2 * mine.shape[0], size), mine.dtype),
        compiler_params=params,
        name="join",
    )(mine, came, *after)


def stage_body(n_cols, nz, n_sum, place_ref, *refs):
    sources, (out_ref, mask_ref, sem) = refs[:4], refs[4:]
    tokens, width = sources[0].shape
    half = width // 2
    copies = [
        pltpu.make_async_copy(
            source.at[:, core_window(place_ref, 0, half, 0, half)], out_ref.at[i], sem.at[i]
        )
        for i, source in enumerate(sources)
    ]
    for copy in copies:
        copy.start()
    mask_ref[...] = far_mask(place_ref[0], place_ref[1], n_cols, nz, n_sum, tokens)
    for copy in copies:
        copy.wait()


def stage(place, arrays, n_cols, nz):
    tokens, width = arrays[0].shape
    n_sum = tokens // BLOCK * SUMMARY
    nkeys = 2 * n_cols * nz * n_sum
    return pl.pallas_call(
        functools.partial(stage_body, n_cols, nz, n_sum),
        in_specs=[in_smem] + [in_hbm] * 4,
        out_specs=[in_vmem] * 2,
        out_shape=[
            jax.ShapeDtypeStruct((4, tokens, width // 2), arrays[0].dtype),
            jax.ShapeDtypeStruct((2 * tokens, nkeys), jnp.float32),
        ],
        scratch_shapes=[pltpu.SemaphoreType.DMA((4,))],
        compiler_params=params,
        cost_estimate=pl.CostEstimate(
            flops=0, bytes_accessed=8 * tokens * width, transcendentals=0
        ),
        name="stage",
    )(place, *[pltpu.with_memory_space_constraint(x, pltpu.HBM) for x in arrays])


def attention_body(n_sum, n_cols, n_skip, first, heads, *refs):
    mine_ref, came_ref, away_mask = refs[:3]
    col_refs = refs[3 : 3 + n_cols]
    outs = refs[3 + n_cols + n_skip :]
    own_ref, sent_ref, near_ref = outs[:3]
    back_refs = outs[3 : 4 + n_cols]
    near_mask = outs[4 + n_cols]
    tokens = mine_ref.shape[1]
    nz = col_refs[0].shape[0]
    n_blocks = tokens // BLOCK
    blocks = [slice(b * BLOCK, (b + 1) * BLOCK) for b in range(2 * n_blocks)]
    near_mask[...] = block_mask()

    def here(to):
        return pl.ds(pl.multiple_of(first * HEAD_DIM + to.start, HEAD_DIM), HEAD_DIM)

    def far_rows(offset, to):
        parts = []
        for ref in col_refs:
            for j in range(nz):
                for core in range(2):
                    row = 2 * core * n_sum + offset
                    parts.append(ref[j, row : row + n_sum, to])
        return jnp.concatenate(parts, axis=0)

    def keep(i, to, b, value):
        if b < n_blocks:
            own_ref[i, blocks[b], here(to)] = value
        else:
            sent_ref[i, blocks[b - n_blocks], here(to)] = value

    def head(to):
        q, k_loc, v_loc, g = (
            jnp.concatenate([ref[i, :, here(to)] for ref in (mine_ref, came_ref)], axis=0)
            for i in range(4)
        )
        k_far = far_rows(0, to)
        v_far = far_rows(n_sum, to)
        mask = near_mask[...]
        s_loc = jnp.concatenate([dot(q[b], k_loc[b], 1, 1) + mask for b in blocks], axis=0)
        s_far = dot(q, k_far, 1, 1) + away_mask[...]
        high = jnp.maximum(
            jnp.max(s_loc, axis=1, keepdims=True), jnp.max(s_far, axis=1, keepdims=True)
        )
        e_loc = jnp.exp2((s_loc - high) * exponent)
        e_far = jnp.exp2((s_far - high) * exponent)
        norm = jnp.sum(e_loc, axis=1, keepdims=True) + jnp.sum(e_far, axis=1, keepdims=True)
        inv = 1.0 / norm
        eb_loc = e_loc.astype(jnp.bfloat16)
        eb_far = e_far.astype(jnp.bfloat16)
        out = jnp.concatenate([dot(eb_loc[b], v_loc[b], 1, 0) for b in blocks], axis=0) + dot(
            eb_far, v_far, 1, 0
        )
        out = (out * inv).astype(jnp.bfloat16)
        gf = g.astype(jnp.float32)
        delta = jnp.sum(gf * out.astype(jnp.float32), axis=1, keepdims=True)
        factor = inv * scaling
        t_loc = jnp.concatenate([dot(g[b], v_loc[b], 1, 1) for b in blocks], axis=0)
        t_loc = (t_loc - delta) * factor
        t_far = (dot(g, v_far, 1, 1) - delta) * factor
        ds_loc = (eb_loc.astype(jnp.float32) * t_loc).astype(jnp.bfloat16)
        ds_far = (eb_far.astype(jnp.float32) * t_far).astype(jnp.bfloat16)
        dq = jnp.concatenate([dot(ds_loc[b], k_loc[b], 1, 0) for b in blocks], axis=0) + dot(
            ds_far, k_far, 1, 0
        )
        dq = dq.astype(jnp.bfloat16)
        gi = (gf * inv).astype(jnp.bfloat16)
        for n, b in enumerate(blocks):
            keep(0, to, n, out[b])
            keep(1, to, n, dq[b])
            for i, (left, right) in enumerate(((ds_loc, q), (eb_loc, gi))):
                part = dot(left[b], right[b], 0, 0)
                keep(2 + i, to, n, part.astype(jnp.bfloat16))
                t, row = n // n_blocks, (i * n_blocks + n % n_blocks) * EDGE
                near_ref[t, row : row + EDGE, to] = part[BLOCK - EDGE :, :]
        dk_far = dot(q, ds_far, 0, 0).astype(jnp.bfloat16).T
        dv_far = dot(gi, eb_far, 0, 0).astype(jnp.bfloat16).T
        row = 0
        for c in range(n_cols):
            for j in range(nz):
                ref, place = back_refs[c], j
                if c == n_cols - 1:
                    ref, place = back_refs[c + j % 2], j // 2
                for core in range(2):
                    to_row = 2 * core * n_sum
                    ref[place, to_row : to_row + n_sum, to] = dk_far[row : row + n_sum]
                    ref[place, to_row + n_sum : to_row + 2 * n_sum, to] = dv_far[row : row + n_sum]
                    row += n_sum

    def turn(step, carried):
        for u in range(unroll):
            h = step * unroll + u
            head(pl.ds(pl.multiple_of(h * HEAD_DIM, HEAD_DIM), HEAD_DIM))
        return carried

    lax.fori_loop(0, heads // unroll, turn, 0)


def attention(mine, came, mask, cols, earlier, after, first, heads):
    tokens = mine.shape[1]
    n_cols = len(cols)
    nz, rows, chunk_width = cols[0].shape
    n_sum = rows // 4
    nkeys = mask.shape[1]
    n_blocks = tokens // BLOCK
    results = jax.ShapeDtypeStruct(mine.shape, mine.dtype)
    near = jax.ShapeDtypeStruct((2, 2 * n_blocks * EDGE, chunk_width), jnp.float32)
    back = jax.ShapeDtypeStruct((nz, rows, chunk_width), jnp.bfloat16)
    half = jax.ShapeDtypeStruct((nz // 2, rows, chunk_width), jnp.bfloat16)
    n_skip = len(earlier) + len(after)
    return pl.pallas_call(
        functools.partial(attention_body, n_sum, n_cols, n_skip, first, heads),
        in_specs=[in_vmem] * (3 + n_cols + n_skip),
        out_specs=[in_vmem] * (4 + n_cols),
        out_shape=[results, results, near] + [back] * (n_cols - 1) + [half] * 2,
        scratch_shapes=[pltpu.VMEM((BLOCK, BLOCK), jnp.float32)],
        input_output_aliases={3 + n_cols + i: i for i in range(len(earlier))},
        compiler_params=params,
        cost_estimate=pl.CostEstimate(
            flops=heads * 24 * tokens * (BLOCK + nkeys) * HEAD_DIM,
            bytes_accessed=heads * HEAD_DIM * (32 * tokens + 8 * nkeys),
            transcendentals=heads * 2 * tokens * (BLOCK + nkeys),
        ),
        name="attention",
    )(mine, came, mask, *cols, *earlier, *after)


def hold_body(*refs):
    pass


def hold(arrays, *after):
    return pl.pallas_call(
        hold_body,
        in_specs=[in_vmem] * (len(arrays) + len(after)),
        out_specs=[in_vmem] * len(arrays),
        out_shape=[jax.ShapeDtypeStruct(a.shape, a.dtype) for a in arrays],
        input_output_aliases={i: i for i in range(len(arrays))},
        compiler_params=params,
        name="hold",
    )(*arrays, *after)


def line_body(at, n_far, own_ref, pair_ref, *refs):
    line_ref = refs[-1]
    line_ref[0] = own_ref[...]
    line_ref[1] = pair_ref[:, at : at + own_ref.shape[1]]
    for j in range(n_far):
        line_ref[2 + j] = refs[j][...]


def stack_line(own, pair, far, at, *after):
    return pl.pallas_call(
        functools.partial(line_body, at, len(far)),
        in_specs=[in_vmem] * (2 + len(far) + len(after)),
        out_specs=in_vmem,
        out_shape=jax.ShapeDtypeStruct((2 + len(far),) + own.shape, own.dtype),
        compiler_params=params,
        name="line",
    )(own, pair, *far, *after)


def pair_sum_body(keep_ref, came_ref, *refs):
    total = keep_ref[...].astype(jnp.float32) + came_ref[...].astype(jnp.float32)
    refs[-1][...] = total.astype(refs[-1].dtype)


def pair_sum(keep, came, *after):
    return pl.pallas_call(
        pair_sum_body,
        in_specs=[in_vmem] * (2 + len(after)),
        out_specs=in_vmem,
        out_shape=jax.ShapeDtypeStruct(keep.shape, keep.dtype),
        compiler_params=params,
        name="pair_sum",
    )(keep, came, *after)


def store_places(totals, out_refs, apart):
    if apart:
        for ref, total in zip(out_refs, totals):
            ref[...] = total.astype(ref.dtype)
        return
    for j, total in enumerate(totals):
        if j % 2 == 0:
            out_refs[j // 2][...] = total.astype(out_refs[j // 2].dtype)
        else:
            out_refs[-1][j // 2] = total.astype(out_refs[-1].dtype)


def places_shapes(n, rows, width, apart):
    kinds = [jnp.float32] + [jnp.bfloat16] * (n - 1)
    if apart:
        return [jax.ShapeDtypeStruct((rows, width), kind) for kind in kinds]
    shapes = [jax.ShapeDtypeStruct((rows, width), kind) for kind in kinds[0::2]]
    return shapes + [jax.ShapeDtypeStruct((n // 2, rows, width), jnp.bfloat16)]


def column_sum_body(n_in, n_after, apart, *refs):
    in_refs, out_refs = refs[:n_in], refs[n_in + n_after :]
    totals = []
    for j in range(in_refs[0].shape[0]):
        total = in_refs[0][j].astype(jnp.float32)
        for came in in_refs[1:-1]:
            total = total + came[j].astype(jnp.float32)
        if j % 2 == 0:
            total = total + in_refs[-1][j // 2].astype(jnp.float32)
        totals.append(total)
    store_places(totals, out_refs, apart)


def column_sum(parts, apart, *after):
    nz, rows, width = parts[0].shape
    shapes = places_shapes(nz, rows, width, apart)
    return pl.pallas_call(
        functools.partial(column_sum_body, len(parts), len(after), apart),
        in_specs=[in_vmem] * (len(parts) + len(after)),
        out_specs=[in_vmem] * len(shapes),
        out_shape=shapes,
        compiler_params=params,
        name="column_sum",
    )(*parts, *after)


def fold_body(n, *refs):
    keeps, came, out_refs = refs[:n], refs[n], refs[n + 1 :]
    totals = [
        keep[...].astype(jnp.float32) + came[i].astype(jnp.float32) for i, keep in enumerate(keeps)
    ]
    store_places(totals, out_refs, False)


def fold(keeps, came):
    n = len(keeps)
    shapes = places_shapes(n, *keeps[0].shape, False)
    return pl.pallas_call(
        functools.partial(fold_body, n),
        in_specs=[in_vmem] * (n + 1),
        out_specs=[in_vmem] * len(shapes),
        out_shape=shapes,
        compiler_params=params,
        name="fold",
    )(*keeps, came)


def edge_body(counts, *refs):
    targets = refs[-2:]
    at = 0
    start = 0
    for count in counts:
        near_ref, *ends = refs[start : start + count]
        start += count
        to = slice(at, at + near_ref.shape[2])
        at += near_ref.shape[2]
        total = ends[0][...]
        for term in ends[1:]:
            total = total + (term[0] if len(term.shape) == 3 else term[...]).astype(jnp.float32)
        rows = total.shape[0] // 2
        for t, target in enumerate(targets):
            for n in range(rows // SUMMARY):
                tile = near_ref[t, n * EDGE : (n + 1) * EDGE, :]
                more = total[t * rows + n * SUMMARY : t * rows + (n + 1) * SUMMARY]
                tile = [tile[: EDGE - SUMMARY], tile[EDGE - SUMMARY :] + more]
                tile = jnp.concatenate(tile, axis=0).astype(target.dtype)
                target[n * EDGE : (n + 1) * EDGE, to] = tile


def edge(chunks, *after):
    width = sum(chunk[0].shape[2] for chunk in chunks)
    shape = jax.ShapeDtypeStruct((chunks[0][0].shape[1], width), jnp.bfloat16)
    terms = [term for chunk in chunks for term in chunk]
    return pl.pallas_call(
        functools.partial(edge_body, [len(chunk) for chunk in chunks]),
        in_specs=[in_vmem] * (len(terms) + len(after)),
        out_specs=[in_vmem] * 2,
        out_shape=[shape] * 2,
        compiler_params=params,
        name="edge",
    )(*terms, *after)


def settle_body(place_ref, own_ref, came_ref, *refs):
    targets, (token_ref, sem) = refs[:4], refs[4:]
    half = own_ref.shape[2]
    copies = []
    for flip, source in enumerate((own_ref, came_ref)):
        to = core_window(place_ref, flip, half, 0, half)
        for i, target in enumerate(targets):
            copies.append(
                pltpu.make_async_copy(source.at[i], target.at[:, to], sem.at[flip, i])
            )
    for copy in copies:
        copy.start()
    token_ref[...] = jnp.zeros(token_ref.shape, token_ref.dtype)
    for copy in copies:
        copy.wait()


def settle(place, own, came):
    tokens, half = own.shape[1:]
    return pl.pallas_call(
        settle_body,
        in_specs=[in_smem, in_vmem, in_vmem],
        out_specs=[in_hbm] * 4 + [in_vmem],
        out_shape=[jax.ShapeDtypeStruct((tokens, 2 * half), own.dtype)] * 4
        + [jax.ShapeDtypeStruct((8, 128), jnp.float32)],
        scratch_shapes=[pltpu.SemaphoreType.DMA((2, 4))],
        compiler_params=params,
        name="settle",
    )(place, own, came)


def finish_body(n_edges, n_blocks, place_ref, *refs):
    edges = refs[2 : 2 + n_edges]
    targets, sem = refs[2 + n_edges : 4 + n_edges], refs[4 + n_edges]
    width = targets[0].shape[1]
    copies = []
    at = 0
    for e, source in enumerate(edges):
        flip = e % 2
        to = core_window(place_ref, flip, width // 2, at, source.shape[1])
        at += flip * source.shape[1]
        for n in range(2 * n_blocks):
            i, b = divmod(n, n_blocks)
            copies.append(
                pltpu.make_async_copy(
                    source.at[pl.ds(n * EDGE, EDGE)],
                    targets[i].at[pl.ds((b + 1) * BLOCK - EDGE, EDGE), to],
                    sem.at[e, n],
                )
            )
    for copy in copies:
        copy.start()
    for copy in copies:
        copy.wait()


def finish(place, dk, dv, edges):
    n_blocks = dk.shape[0] // BLOCK
    return pl.pallas_call(
        functools.partial(finish_body, len(edges), n_blocks),
        in_specs=[in_smem] + [in_hbm] * 2 + [in_vmem] * len(edges),
        out_specs=[in_hbm] * 2,
        out_shape=[jax.ShapeDtypeStruct(dk.shape, dk.dtype)] * 2,
        scratch_shapes=[pltpu.SemaphoreType.DMA((len(edges), 2 * n_blocks))],
        input_output_aliases={1: 0, 2: 1},
        compiler_params=params,
        name="finish",
    )(place, dk, dv, *edges)


def on_device(n_seq, nz, queries, keys_in, values_in, cotangent):
    n_cols = n_seq // 2
    n_chunks = len(chunk_heads)
    firsts = [sum(chunk_heads[:c]) for c in range(n_chunks)]

    def over_z(array, bits):
        return lax.ppermute(array, "head", [(i, i ^ bits) for i in range(nz)])

    def over_seq(array, bits):
        return lax.ppermute(array, "seq", [(i, i ^ bits) for i in range(n_seq)])

    def swap_far(pieces):
        return [over_z(pieces[j], j) for j in reversed(range(2, nz))][::-1]

    def swap_columns(parts):
        return [over_seq(parts[c], 2 * c) for c in reversed(range(1, len(parts)))][::-1]

    place = jnp.stack([lax.axis_index("seq"), lax.axis_index("head")]).astype(jnp.int32)
    arrays = (queries, keys_in, values_in, cotangent)
    mine, other, part = pack(place, arrays)
    came = over_seq(other, 1)
    pair = over_z(join(mine, came, 0, mine.shape[1]), 1)
    ours, mask = stage(place, arrays, n_cols, nz)
    columns = []
    theirs = over_seq(hold([part], came)[0], 1)
    for c in range(n_chunks):
        width = chunk_heads[c] * HEAD_DIM
        at = firsts[c] * HEAD_DIM
        own = join(mine, came, at, width, *[cols[0] for cols in columns[-1:]])
        far = swap_far([own] * nz)
        line = stack_line(own, pair, far, at, *([cols[-1] for cols in columns[-1:]] or [theirs, mask]))
        columns.append([line] + swap_columns([line] * n_cols))

    results = ()
    chunks = []
    back = None
    for c in range(n_chunks):
        made = attention(
            ours,
            theirs,
            mask,
            columns[c],
            results,
            [cols[0] for cols in columns[c + 1 : c + 2]] + ([paired] if c else []),
            firsts[c],
            chunk_heads[c],
        )
        results, near, parts = made[:2], made[2], list(made[3:])
        waits = columns[c + 1] if c + 1 < n_chunks else [None] * n_cols
        if back is not None:
            waits = back[1]
        moved = [hold([parts[i]], waits[i])[0] for i in range(1, n_cols - 1)]
        give = hold([parts[n_cols]], waits[n_cols - 2])[0] if c else parts[n_cols]
        after = []
        if back is not None:
            *keeps, give_z = column_sum(back[1], False, near)
            after = keeps[:1]
        paired = pair_sum(parts[n_cols - 1], over_z(give, 1), *after)
        last = over_seq(paired, 2 * (n_cols - 1))
        moved = swap_columns(parts[:1] + moved) + [last]
        if back is not None:
            bits = 1
            while len(keeps) > 1:
                *keeps, give_z = fold(keeps, over_z(give_z, bits))
                bits *= 2
            chunks.append([back[0], keeps[0], over_z(give_z, bits)])
        back = near, parts[:1] + moved
    ends = column_sum(back[1], True, chunks[-1][1])
    chunks.append([back[0], ends[0], over_z(ends[1], 1)] + swap_far(ends))
    own, sent = results
    (sent,) = hold([sent], ends[0])
    *results, mark = settle(place, own, over_seq(sent, 1))
    own, away = edge(chunks, mark)
    attended, grad_queries, dk, dv = results
    edges = [own, over_seq(away, 1)]
    grad_keys, grad_values = finish(place, dk, dv, edges)
    return (attended, grad_queries, grad_keys, grad_values)


def solution(mesh):
    spec = P(("seq", "head"), None)
    return jax.shard_map(
        functools.partial(on_device, mesh.shape["seq"], mesh.shape["head"]),
        mesh=mesh,
        in_specs=(spec,) * 4,
        out_specs=(spec,) * 4,
        check_vma=False,
    )
```

```python
import functools
import math

import jax
import jax.numpy as jnp
from jax import lax
from jax.experimental import pallas as pl
from jax.experimental.pallas import tpu as pltpu
from jax.sharding import PartitionSpec as P

HEADS = 16
HEAD_DIM = 128
BLOCK = 128
SUMMARY = 8
EDGE = 16

neg_fill = -1e30
scaling = 1.0 / math.sqrt(HEAD_DIM)
exponent = scaling / math.log(2.0)
chunk_heads = (4, 4)
unroll = 2
vmem_bytes = 40 * 1024 * 1024
in_vmem = pl.BlockSpec(memory_space=pltpu.VMEM)
in_hbm = pl.BlockSpec(memory_space=pltpu.HBM)
in_smem = pl.BlockSpec(memory_space=pltpu.SMEM)
params = pltpu.CompilerParams(vmem_limit_bytes=vmem_bytes)


def dot(left, right, left_dim, right_dim):
    return lax.dot_general(
        left, right, (((left_dim,), (right_dim,)), ((), ())), preferred_element_type=jnp.float32
    )


def block_mask():
    key = lax.broadcasted_iota(jnp.int32, (BLOCK, BLOCK), 1)
    query = lax.broadcasted_iota(jnp.int32, (BLOCK, BLOCK), 0)
    return jnp.where(key <= query, 0.0, neg_fill)


def far_mask(seq_pos, z_pos, n_cols, nz, n_sum, tokens):
    shape = (2 * tokens, n_cols * nz * 2 * n_sum)
    key = lax.broadcasted_iota(jnp.int32, shape, 1)
    query = lax.broadcasted_iota(jnp.int32, shape, 0)
    piece = key // n_sum
    column = piece // (2 * nz)
    source = (seq_pos ^ (2 * column + piece % 2)) * nz + (z_pos ^ ((piece // 2) % nz))
    here = (seq_pos ^ (query // tokens)) * nz + z_pos
    before = (key % n_sum) // SUMMARY < (query % tokens) // BLOCK
    return jnp.where((source < here) | ((source == here) & before), 0.0, neg_fill)


def core_window(place_ref, flip, half, at, size):
    core = (place_ref[0] + flip) % 2
    return pl.ds(pl.multiple_of(core * half + at, HEAD_DIM), size)


def pack_body(place_ref, *refs):
    sources, (mine_ref, other_ref, away_ref, tiles, tile_sem, sem) = refs[:4], refs[4:]
    tokens, width = sources[0].shape
    n_blocks = tokens // BLOCK
    half = width // 2
    copies = []
    for i, source in enumerate(sources[1:3]):
        for b in range(n_blocks):
            row = i * n_blocks + b
            tile = pl.ds((b + 1) * BLOCK - EDGE, EDGE)
            copies.append(pltpu.make_async_copy(source.at[tile, :], tiles.at[row], tile_sem.at[row]))
    columns = [
        pltpu.make_async_copy(
            source.at[:, core_window(place_ref, 1, half, 0, half)], away_ref.at[i], sem.at[i]
        )
        for i, source in enumerate(sources)
    ]
    for copy in copies + columns:
        copy.start()
    for copy in copies:
        copy.wait()
    for flip, target in enumerate((mine_ref, other_ref)):
        to = core_window(place_ref, flip, half, 0, half)
        rows = [tiles[row, EDGE - SUMMARY :, to] for row in range(2 * n_blocks)]
        target[...] = jnp.concatenate(rows, axis=0)
    for copy in columns:
        copy.wait()


def pack(place, arrays):
    tokens, width = arrays[0].shape
    kind = arrays[0].dtype
    n_blocks = tokens // BLOCK
    shape = jax.ShapeDtypeStruct((2 * n_blocks * SUMMARY, width // 2), kind)
    return pl.pallas_call(
        pack_body,
        in_specs=[in_smem] + [in_hbm] * 4,
        out_specs=[in_vmem] * 3,
        out_shape=[shape] * 2 + [jax.ShapeDtypeStruct((4, tokens, width // 2), kind)],
        scratch_shapes=[
            pltpu.VMEM((2 * n_blocks, EDGE, width), kind),
            pltpu.SemaphoreType.DMA((2 * n_blocks,)),
            pltpu.SemaphoreType.DMA((4,)),
        ],
        compiler_params=params,
        name="pack",
    )(place, *[pltpu.with_memory_space_constraint(x, pltpu.HBM) for x in arrays])


def join_body(at, mine_ref, came_ref, *refs):
    ref = refs[-1]
    rows, width = mine_ref.shape[0], ref.shape[1]
    ref[:rows] = mine_ref[:, at : at + width]
    ref[rows:] = came_ref[:, at : at + width]


def join(mine, came, at, size, *after):
    return pl.pallas_call(
        functools.partial(join_body, at),
        in_specs=[in_vmem] * (2 + len(after)),
        out_specs=in_vmem,
        out_shape=jax.ShapeDtypeStruct((2 * mine.shape[0], size), mine.dtype),
        compiler_params=params,
        name="join",
    )(mine, came, *after)


def stage_body(n_cols, nz, n_sum, place_ref, *refs):
    sources, (out_ref, mask_ref, sem) = refs[:4], refs[4:]
    tokens, width = sources[0].shape
    half = width // 2
    copies = [
        pltpu.make_async_copy(
            source.at[:, core_window(place_ref, 0, half, 0, half)], out_ref.at[i], sem.at[i]
        )
        for i, source in enumerate(sources)
    ]
    for copy in copies:
        copy.start()
    mask_ref[...] = far_mask(place_ref[0], place_ref[1], n_cols, nz, n_sum, tokens)
    for copy in copies:
        copy.wait()


def stage(place, arrays, n_cols, nz):
    tokens, width = arrays[0].shape
    n_sum = tokens // BLOCK * SUMMARY
    nkeys = 2 * n_cols * nz * n_sum
    return pl.pallas_call(
        functools.partial(stage_body, n_cols, nz, n_sum),
        in_specs=[in_smem] + [in_hbm] * 4,
        out_specs=[in_vmem] * 2,
        out_shape=[
            jax.ShapeDtypeStruct((4, tokens, width // 2), arrays[0].dtype),
            jax.ShapeDtypeStruct((2 * tokens, nkeys), jnp.float32),
        ],
        scratch_shapes=[pltpu.SemaphoreType.DMA((4,))],
        compiler_params=params,
        cost_estimate=pl.CostEstimate(
            flops=0, bytes_accessed=8 * tokens * width, transcendentals=0
        ),
        name="stage",
    )(place, *[pltpu.with_memory_space_constraint(x, pltpu.HBM) for x in arrays])


def attention_body(n_sum, n_cols, n_skip, first, heads, *refs):
    mine_ref, came_ref, away_mask = refs[:3]
    col_refs = refs[3 : 3 + n_cols]
    outs = refs[3 + n_cols + n_skip :]
    own_ref, sent_ref, near_ref = outs[:3]
    back_refs = outs[3 : 4 + n_cols]
    near_mask = outs[4 + n_cols]
    tokens = mine_ref.shape[1]
    nz = col_refs[0].shape[0]
    n_blocks = tokens // BLOCK
    blocks = [slice(b * BLOCK, (b + 1) * BLOCK) for b in range(2 * n_blocks)]
    near_mask[...] = block_mask()

    def here(to):
        return pl.ds(pl.multiple_of(first * HEAD_DIM + to.start, HEAD_DIM), HEAD_DIM)

    def far_rows(offset, to):
        parts = []
        for ref in col_refs:
            for j in range(nz):
                for core in range(2):
                    row = 2 * core * n_sum + offset
                    parts.append(ref[j, row : row + n_sum, to])
        return jnp.concatenate(parts, axis=0)

    def keep(i, to, b, value):
        if b < n_blocks:
            own_ref[i, blocks[b], here(to)] = value
        else:
            sent_ref[i, blocks[b - n_blocks], here(to)] = value

    def head(to):
        q, k_loc, v_loc, g = (
            jnp.concatenate([ref[i, :, here(to)] for ref in (mine_ref, came_ref)], axis=0)
            for i in range(4)
        )
        k_far = far_rows(0, to)
        v_far = far_rows(n_sum, to)
        mask = near_mask[...]
        s_loc = jnp.concatenate([dot(q[b], k_loc[b], 1, 1) + mask for b in blocks], axis=0)
        s_far = dot(q, k_far, 1, 1) + away_mask[...]
        high = jnp.maximum(
            jnp.max(s_loc, axis=1, keepdims=True), jnp.max(s_far, axis=1, keepdims=True)
        )
        e_loc = jnp.exp2((s_loc - high) * exponent)
        e_far = jnp.exp2((s_far - high) * exponent)
        norm = jnp.sum(e_loc, axis=1, keepdims=True) + jnp.sum(e_far, axis=1, keepdims=True)
        inv = 1.0 / norm
        eb_loc = e_loc.astype(jnp.bfloat16)
        eb_far = e_far.astype(jnp.bfloat16)
        out = jnp.concatenate([dot(eb_loc[b], v_loc[b], 1, 0) for b in blocks], axis=0) + dot(
            eb_far, v_far, 1, 0
        )
        out = (out * inv).astype(jnp.bfloat16)
        gf = g.astype(jnp.float32)
        delta = jnp.sum(gf * out.astype(jnp.float32), axis=1, keepdims=True)
        factor = inv * scaling
        t_loc = jnp.concatenate([dot(g[b], v_loc[b], 1, 1) for b in blocks], axis=0)
        t_loc = (t_loc - delta) * factor
        t_far = (dot(g, v_far, 1, 1) - delta) * factor
        ds_loc = (eb_loc.astype(jnp.float32) * t_loc).astype(jnp.bfloat16)
        ds_far = (eb_far.astype(jnp.float32) * t_far).astype(jnp.bfloat16)
        dq = jnp.concatenate([dot(ds_loc[b], k_loc[b], 1, 0) for b in blocks], axis=0) + dot(
            ds_far, k_far, 1, 0
        )
        dq = dq.astype(jnp.bfloat16)
        gi = (gf * inv).astype(jnp.bfloat16)
        for n, b in enumerate(blocks):
            keep(0, to, n, out[b])
            keep(1, to, n, dq[b])
            for i, (left, right) in enumerate(((ds_loc, q), (eb_loc, gi))):
                part = dot(left[b], right[b], 0, 0)
                keep(2 + i, to, n, part.astype(jnp.bfloat16))
                t, row = n // n_blocks, (i * n_blocks + n % n_blocks) * EDGE
                near_ref[t, row : row + EDGE, to] = part[BLOCK - EDGE :, :]
        dk_far = dot(q, ds_far, 0, 0).astype(jnp.bfloat16).T
        dv_far = dot(gi, eb_far, 0, 0).astype(jnp.bfloat16).T
        row = 0
        for c in range(n_cols):
            for j in range(nz):
                ref, place = back_refs[c], j
                if c == n_cols - 1:
                    ref, place = back_refs[c + j % 2], j // 2
                for core in range(2):
                    to_row = 2 * core * n_sum
                    ref[place, to_row : to_row + n_sum, to] = dk_far[row : row + n_sum]
                    ref[place, to_row + n_sum : to_row + 2 * n_sum, to] = dv_far[row : row + n_sum]
                    row += n_sum

    def turn(step, carried):
        for u in range(unroll):
            h = step * unroll + u
            head(pl.ds(pl.multiple_of(h * HEAD_DIM, HEAD_DIM), HEAD_DIM))
        return carried

    lax.fori_loop(0, heads // unroll, turn, 0)


def attention(mine, came, mask, cols, earlier, after, first, heads):
    tokens = mine.shape[1]
    n_cols = len(cols)
    nz, rows, chunk_width = cols[0].shape
    n_sum = rows // 4
    nkeys = mask.shape[1]
    n_blocks = tokens // BLOCK
    results = jax.ShapeDtypeStruct(mine.shape, mine.dtype)
    near = jax.ShapeDtypeStruct((2, 2 * n_blocks * EDGE, chunk_width), jnp.float32)
    back = jax.ShapeDtypeStruct((nz, rows, chunk_width), jnp.bfloat16)
    half = jax.ShapeDtypeStruct((nz // 2, rows, chunk_width), jnp.bfloat16)
    n_skip = len(earlier) + len(after)
    return pl.pallas_call(
        functools.partial(attention_body, n_sum, n_cols, n_skip, first, heads),
        in_specs=[in_vmem] * (3 + n_cols + n_skip),
        out_specs=[in_vmem] * (4 + n_cols),
        out_shape=[results, results, near] + [back] * (n_cols - 1) + [half] * 2,
        scratch_shapes=[pltpu.VMEM((BLOCK, BLOCK), jnp.float32)],
        input_output_aliases={3 + n_cols + i: i for i in range(len(earlier))},
        compiler_params=params,
        cost_estimate=pl.CostEstimate(
            flops=heads * 24 * tokens * (BLOCK + nkeys) * HEAD_DIM,
            bytes_accessed=heads * HEAD_DIM * (32 * tokens + 8 * nkeys),
            transcendentals=heads * 2 * tokens * (BLOCK + nkeys),
        ),
        name="attention",
    )(mine, came, mask, *cols, *earlier, *after)


def hold_body(*refs):
    pass


def hold(arrays, *after):
    return pl.pallas_call(
        hold_body,
        in_specs=[in_vmem] * (len(arrays) + len(after)),
        out_specs=[in_vmem] * len(arrays),
        out_shape=[jax.ShapeDtypeStruct(a.shape, a.dtype) for a in arrays],
        input_output_aliases={i: i for i in range(len(arrays))},
        compiler_params=params,
        name="hold",
    )(*arrays, *after)


def line_body(at, n_far, own_ref, pair_ref, *refs):
    line_ref = refs[-1]
    line_ref[0] = own_ref[...]
    line_ref[1] = pair_ref[:, at : at + own_ref.shape[1]]
    for j in range(n_far):
        line_ref[2 + j] = refs[j][...]


def stack_line(own, pair, far, at, *after):
    return pl.pallas_call(
        functools.partial(line_body, at, len(far)),
        in_specs=[in_vmem] * (2 + len(far) + len(after)),
        out_specs=in_vmem,
        out_shape=jax.ShapeDtypeStruct((2 + len(far),) + own.shape, own.dtype),
        compiler_params=params,
        name="line",
    )(own, pair, *far, *after)


def pair_sum_body(keep_ref, came_ref, *refs):
    total = keep_ref[...].astype(jnp.float32) + came_ref[...].astype(jnp.float32)
    refs[-1][...] = total.astype(refs[-1].dtype)


def pair_sum(keep, came, *after):
    return pl.pallas_call(
        pair_sum_body,
        in_specs=[in_vmem] * (2 + len(after)),
        out_specs=in_vmem,
        out_shape=jax.ShapeDtypeStruct(keep.shape, keep.dtype),
        compiler_params=params,
        name="pair_sum",
    )(keep, came, *after)


def store_places(totals, out_refs, apart):
    if apart:
        for ref, total in zip(out_refs, totals):
            ref[...] = total.astype(ref.dtype)
        return
    for j, total in enumerate(totals):
        if j % 2 == 0:
            out_refs[j // 2][...] = total.astype(out_refs[j // 2].dtype)
        else:
            out_refs[-1][j // 2] = total.astype(out_refs[-1].dtype)


def places_shapes(n, rows, width, apart):
    kinds = [jnp.float32] + [jnp.bfloat16] * (n - 1)
    if apart:
        return [jax.ShapeDtypeStruct((rows, width), kind) for kind in kinds]
    shapes = [jax.ShapeDtypeStruct((rows, width), kind) for kind in kinds[0::2]]
    return shapes + [jax.ShapeDtypeStruct((n // 2, rows, width), jnp.bfloat16)]


def column_sum_body(n_in, n_after, apart, *refs):
    in_refs, out_refs = refs[:n_in], refs[n_in + n_after :]
    totals = []
    for j in range(in_refs[0].shape[0]):
        total = in_refs[0][j].astype(jnp.float32)
        for came in in_refs[1:-1]:
            total = total + came[j].astype(jnp.float32)
        if j % 2 == 0:
            total = total + in_refs[-1][j // 2].astype(jnp.float32)
        totals.append(total)
    store_places(totals, out_refs, apart)


def column_sum(parts, apart, *after):
    nz, rows, width = parts[0].shape
    shapes = places_shapes(nz, rows, width, apart)
    return pl.pallas_call(
        functools.partial(column_sum_body, len(parts), len(after), apart),
        in_specs=[in_vmem] * (len(parts) + len(after)),
        out_specs=[in_vmem] * len(shapes),
        out_shape=shapes,
        compiler_params=params,
        name="column_sum",
    )(*parts, *after)


def total_body(n, *refs):
    total = refs[0][...]
    for ref in refs[1:n]:
        total = total + ref[...].astype(jnp.float32)
    refs[-1][...] = total


def total_of(parts, *after):
    return pl.pallas_call(
        functools.partial(total_body, len(parts)),
        in_specs=[in_vmem] * (len(parts) + len(after)),
        out_specs=in_vmem,
        out_shape=jax.ShapeDtypeStruct(parts[0].shape, jnp.float32),
        compiler_params=params,
        name="total",
    )(*parts, *after)


def fold_body(n, *refs):
    keeps, came, out_refs = refs[:n], refs[n], refs[n + 1 :]
    totals = [
        keep[...].astype(jnp.float32) + came[i].astype(jnp.float32) for i, keep in enumerate(keeps)
    ]
    store_places(totals, out_refs, False)


def fold(keeps, came):
    n = len(keeps)
    shapes = places_shapes(n, *keeps[0].shape, False)
    return pl.pallas_call(
        functools.partial(fold_body, n),
        in_specs=[in_vmem] * (n + 1),
        out_specs=[in_vmem] * len(shapes),
        out_shape=shapes,
        compiler_params=params,
        name="fold",
    )(*keeps, came)


def edge_body(counts, *refs):
    targets = refs[-2:]
    at = 0
    start = 0
    for count in counts:
        near_ref, *ends = refs[start : start + count]
        start += count
        to = slice(at, at + near_ref.shape[2])
        at += near_ref.shape[2]
        total = ends[0][...]
        for term in ends[1:]:
            total = total + (term[0] if len(term.shape) == 3 else term[...]).astype(jnp.float32)
        rows = total.shape[0] // 2
        for t, target in enumerate(targets):
            for n in range(rows // SUMMARY):
                tile = near_ref[t, n * EDGE : (n + 1) * EDGE, :]
                more = total[t * rows + n * SUMMARY : t * rows + (n + 1) * SUMMARY]
                tile = [tile[: EDGE - SUMMARY], tile[EDGE - SUMMARY :] + more]
                tile = jnp.concatenate(tile, axis=0).astype(target.dtype)
                target[n * EDGE : (n + 1) * EDGE, to] = tile


def edge(chunks, *after):
    width = sum(chunk[0].shape[2] for chunk in chunks)
    shape = jax.ShapeDtypeStruct((chunks[0][0].shape[1], width), jnp.bfloat16)
    terms = [term for chunk in chunks for term in chunk]
    return pl.pallas_call(
        functools.partial(edge_body, [len(chunk) for chunk in chunks]),
        in_specs=[in_vmem] * (len(terms) + len(after)),
        out_specs=[in_vmem] * 2,
        out_shape=[shape] * 2,
        compiler_params=params,
        name="edge",
    )(*terms, *after)


def settle_body(place_ref, own_ref, came_ref, *refs):
    targets, (token_ref, sem) = refs[:4], refs[4:]
    half = own_ref.shape[2]
    copies = []
    for flip, source in enumerate((own_ref, came_ref)):
        to = core_window(place_ref, flip, half, 0, half)
        for i, target in enumerate(targets):
            copies.append(
                pltpu.make_async_copy(source.at[i], target.at[:, to], sem.at[flip, i])
            )
    for copy in copies:
        copy.start()
    token_ref[...] = jnp.zeros(token_ref.shape, token_ref.dtype)
    for copy in copies:
        copy.wait()


def settle(place, own, came):
    tokens, half = own.shape[1:]
    return pl.pallas_call(
        settle_body,
        in_specs=[in_smem, in_vmem, in_vmem],
        out_specs=[in_hbm] * 4 + [in_vmem],
        out_shape=[jax.ShapeDtypeStruct((tokens, 2 * half), own.dtype)] * 4
        + [jax.ShapeDtypeStruct((8, 128), jnp.float32)],
        scratch_shapes=[pltpu.SemaphoreType.DMA((2, 4))],
        compiler_params=params,
        name="settle",
    )(place, own, came)


def finish_body(n_edges, n_blocks, place_ref, *refs):
    edges = refs[2 : 2 + n_edges]
    targets, sem = refs[2 + n_edges : 4 + n_edges], refs[4 + n_edges]
    width = targets[0].shape[1]
    copies = []
    at = 0
    for e, source in enumerate(edges):
        flip = e % 2
        to = core_window(place_ref, flip, width // 2, at, source.shape[1])
        at += flip * source.shape[1]
        for n in range(2 * n_blocks):
            i, b = divmod(n, n_blocks)
            copies.append(
                pltpu.make_async_copy(
                    source.at[pl.ds(n * EDGE, EDGE)],
                    targets[i].at[pl.ds((b + 1) * BLOCK - EDGE, EDGE), to],
                    sem.at[e, n],
                )
            )
    for copy in copies:
        copy.start()
    for copy in copies:
        copy.wait()


def finish(place, dk, dv, edges):
    n_blocks = dk.shape[0] // BLOCK
    return pl.pallas_call(
        functools.partial(finish_body, len(edges), n_blocks),
        in_specs=[in_smem] + [in_hbm] * 2 + [in_vmem] * len(edges),
        out_specs=[in_hbm] * 2,
        out_shape=[jax.ShapeDtypeStruct(dk.shape, dk.dtype)] * 2,
        scratch_shapes=[pltpu.SemaphoreType.DMA((len(edges), 2 * n_blocks))],
        input_output_aliases={1: 0, 2: 1},
        compiler_params=params,
        name="finish",
    )(place, dk, dv, *edges)


def on_device(n_seq, nz, queries, keys_in, values_in, cotangent):
    n_cols = n_seq // 2
    n_chunks = len(chunk_heads)
    firsts = [sum(chunk_heads[:c]) for c in range(n_chunks)]

    def over_z(array, bits):
        return lax.ppermute(array, "head", [(i, i ^ bits) for i in range(nz)])

    def over_seq(array, bits):
        return lax.ppermute(array, "seq", [(i, i ^ bits) for i in range(n_seq)])

    def swap_far(pieces):
        return [over_z(pieces[j], j) for j in reversed(range(2, nz))][::-1]

    def swap_columns(parts):
        return [over_seq(parts[c], 2 * c) for c in reversed(range(1, len(parts)))][::-1]

    place = jnp.stack([lax.axis_index("seq"), lax.axis_index("head")]).astype(jnp.int32)
    arrays = (queries, keys_in, values_in, cotangent)
    mine, other, part = pack(place, arrays)
    came = over_seq(other, 1)
    pair = over_z(join(mine, came, 0, mine.shape[1]), 1)
    ours, mask = stage(place, arrays, n_cols, nz)
    columns = []
    theirs = over_seq(hold([part], came)[0], 1)
    for c in range(n_chunks):
        width = chunk_heads[c] * HEAD_DIM
        at = firsts[c] * HEAD_DIM
        own = join(mine, came, at, width, *[cols[0] for cols in columns[-1:]])
        far = swap_far([own] * nz)
        line = stack_line(own, pair, far, at, *([cols[-1] for cols in columns[-1:]] or [theirs, mask]))
        columns.append([line] + swap_columns([line] * n_cols))

    results = ()
    chunks = []
    back = None
    for c in range(n_chunks):
        made = attention(
            ours,
            theirs,
            mask,
            columns[c],
            results,
            [cols[0] for cols in columns[c + 1 : c + 2]] + ([paired] if c else []),
            firsts[c],
            chunk_heads[c],
        )
        results, near, parts = made[:2], made[2], list(made[3:])
        waits = columns[c + 1] if c + 1 < n_chunks else [None] * n_cols
        if back is not None:
            waits = back[1]
        moved = [hold([parts[i]], waits[i])[0] for i in range(1, n_cols - 1)]
        give = hold([parts[n_cols]], waits[n_cols - 2])[0] if c else parts[n_cols]
        after = []
        if back is not None:
            *keeps, give_z = column_sum(back[1], False, near)
            after = keeps[:1]
        paired = pair_sum(parts[n_cols - 1], over_z(give, 1), *after)
        last = over_seq(paired, 2 * (n_cols - 1))
        moved = swap_columns(parts[:1] + moved) + [last]
        if back is not None:
            bits = 1
            while len(keeps) > 1:
                *keeps, give_z = fold(keeps, over_z(give_z, bits))
                bits *= 2
            chunks.append([back[0], keeps[0], over_z(give_z, bits)])
        back = near, parts[:1] + moved
    ends = column_sum(back[1], True, *chunks[-1][2:])
    pair, far = over_z(ends[1], 1), swap_far(ends)
    own, sent = results
    (sent,) = hold([sent], ends[0])
    *results, mark = settle(place, own, over_seq(sent, 1))
    chunks.append([back[0], total_of([ends[0]] + far, mark), pair])
    own, away = edge(chunks)
    attended, grad_queries, dk, dv = results
    edges = [own, over_seq(away, 1)]
    grad_keys, grad_values = finish(place, dk, dv, edges)
    return (attended, grad_queries, grad_keys, grad_values)


def solution(mesh):
    spec = P(("seq", "head"), None)
    return jax.shard_map(
        functools.partial(on_device, mesh.shape["seq"], mesh.shape["head"]),
        mesh=mesh,
        in_specs=(spec,) * 4,
        out_specs=(spec,) * 4,
        check_vma=False,
    )
```

```python
import functools
import math

import jax
import jax.numpy as jnp
from jax import lax
from jax.experimental import pallas as pl
from jax.experimental.pallas import tpu as pltpu
from jax.sharding import PartitionSpec as P

HEADS = 16
HEAD_DIM = 128
BLOCK = 128
SUMMARY = 8
EDGE = 16

neg_fill = -1e30
scaling = 1.0 / math.sqrt(HEAD_DIM)
exponent = scaling / math.log(2.0)
chunk_heads = (4, 4)
unroll = 2
vmem_bytes = 40 * 1024 * 1024
in_vmem = pl.BlockSpec(memory_space=pltpu.VMEM)
in_hbm = pl.BlockSpec(memory_space=pltpu.HBM)
in_smem = pl.BlockSpec(memory_space=pltpu.SMEM)
params = pltpu.CompilerParams(vmem_limit_bytes=vmem_bytes)


def dot(left, right, left_dim, right_dim):
    return lax.dot_general(
        left, right, (((left_dim,), (right_dim,)), ((), ())), preferred_element_type=jnp.float32
    )


def block_mask():
    key = lax.broadcasted_iota(jnp.int32, (BLOCK, BLOCK), 1)
    query = lax.broadcasted_iota(jnp.int32, (BLOCK, BLOCK), 0)
    return jnp.where(key <= query, 0.0, neg_fill)


def far_mask(seq_pos, z_pos, n_cols, nz, n_sum, tokens):
    shape = (2 * tokens, n_cols * nz * 2 * n_sum)
    key = lax.broadcasted_iota(jnp.int32, shape, 1)
    query = lax.broadcasted_iota(jnp.int32, shape, 0)
    piece = key // n_sum
    column = piece // (2 * nz)
    source = (seq_pos ^ (2 * column + piece % 2)) * nz + (z_pos ^ ((piece // 2) % nz))
    here = (seq_pos ^ (query // tokens)) * nz + z_pos
    before = (key % n_sum) // SUMMARY < (query % tokens) // BLOCK
    return jnp.where((source < here) | ((source == here) & before), 0.0, neg_fill)


def core_window(place_ref, flip, half, at, size):
    core = (place_ref[0] + flip) % 2
    return pl.ds(pl.multiple_of(core * half + at, HEAD_DIM), size)


def summary_rows(matrix):
    blocks = range(BLOCK, matrix.shape[0] + 1, BLOCK)
    return [lax.slice_in_dim(matrix, end - SUMMARY, end) for end in blocks]


def away_body(at, place_ref, *refs):
    sources, (out_ref, side_ref, sem) = refs[:4], refs[-3:]
    half = sources[0].shape[1] // 2
    copies = [
        pltpu.make_async_copy(
            source.at[:, core_window(place_ref, 1, half, at, out_ref.shape[2])],
            out_ref.at[i],
            sem.at[i],
        )
        for i, source in enumerate(sources)
    ]
    for copy in copies:
        copy.start()
    side_ref[...] = jnp.full(side_ref.shape, place_ref[0] % 2, jnp.int32).astype(jnp.float32)
    for copy in copies:
        copy.wait()


def away_heads(place, arrays, at, size, *after):
    tokens = arrays[0].shape[0]
    return pl.pallas_call(
        functools.partial(away_body, at),
        in_specs=[in_smem] + [in_hbm] * 4 + [in_vmem] * len(after),
        out_specs=[in_vmem] * 2,
        out_shape=[
            jax.ShapeDtypeStruct((4, tokens, size), arrays[0].dtype),
            jax.ShapeDtypeStruct((8, 128), jnp.float32),
        ],
        scratch_shapes=[pltpu.SemaphoreType.DMA((4,))],
        compiler_params=params,
        cost_estimate=pl.CostEstimate(
            flops=0, bytes_accessed=16 * tokens * size, transcendentals=0
        ),
        name="away_heads",
    )(place, *[pltpu.with_memory_space_constraint(x, pltpu.HBM) for x in arrays], *after)


def join_body(at, side_ref, mine_ref, came_ref, *refs):
    ref = refs[-1]
    rows, width = mine_ref.shape
    second = jnp.broadcast_to(side_ref[:1, :1], (rows, ref.shape[1])) > 0.5
    for i, source in enumerate((mine_ref, came_ref)):
        low, high = (
            source[:, start : start + ref.shape[1]].astype(jnp.float32)
            for start in (at, width // 2 + at)
        )
        ref[i * rows : (i + 1) * rows] = jnp.where(second, high, low).astype(ref.dtype)


def join(side, mine, came, at, size, *after):
    return pl.pallas_call(
        functools.partial(join_body, at),
        in_specs=[in_vmem] * (3 + len(after)),
        out_specs=in_vmem,
        out_shape=jax.ShapeDtypeStruct((2 * mine.shape[0], size), mine.dtype),
        compiler_params=params,
        name="join",
    )(side, mine, came, *after)


def stage_body(n_cols, nz, n_sum, place_ref, *refs):
    sources, (out_ref, mask_ref, sem) = refs[:4], refs[4:]
    tokens, width = sources[0].shape
    half = width // 2
    copies = [
        pltpu.make_async_copy(
            source.at[:, core_window(place_ref, 0, half, 0, half)], out_ref.at[i], sem.at[i]
        )
        for i, source in enumerate(sources)
    ]
    for copy in copies:
        copy.start()
    mask_ref[...] = far_mask(place_ref[0], place_ref[1], n_cols, nz, n_sum, tokens)
    for copy in copies:
        copy.wait()


def stage(place, arrays, n_cols, nz):
    tokens, width = arrays[0].shape
    n_sum = tokens // BLOCK * SUMMARY
    nkeys = 2 * n_cols * nz * n_sum
    return pl.pallas_call(
        functools.partial(stage_body, n_cols, nz, n_sum),
        in_specs=[in_smem] + [in_hbm] * 4,
        out_specs=[in_vmem] * 2,
        out_shape=[
            jax.ShapeDtypeStruct((4, tokens, width // 2), arrays[0].dtype),
            jax.ShapeDtypeStruct((2 * tokens, nkeys), jnp.float32),
        ],
        scratch_shapes=[pltpu.SemaphoreType.DMA((4,))],
        compiler_params=params,
        cost_estimate=pl.CostEstimate(
            flops=0, bytes_accessed=8 * tokens * width, transcendentals=0
        ),
        name="stage",
    )(place, *[pltpu.with_memory_space_constraint(x, pltpu.HBM) for x in arrays])


def attention_body(n_sum, n_cols, n_skip, first, heads, *refs):
    mine_ref, came_ref, away_mask = refs[:3]
    col_refs = refs[3 : 3 + n_cols]
    outs = refs[3 + n_cols + n_skip :]
    own_ref, sent_ref, near_ref = outs[:3]
    back_refs = outs[3 : 4 + n_cols]
    near_mask = outs[4 + n_cols]
    tokens = mine_ref.shape[1]
    nz = col_refs[0].shape[0]
    n_blocks = tokens // BLOCK
    blocks = [slice(b * BLOCK, (b + 1) * BLOCK) for b in range(2 * n_blocks)]
    near_mask[...] = block_mask()

    def here(to):
        return pl.ds(pl.multiple_of(first * HEAD_DIM + to.start, HEAD_DIM), HEAD_DIM)

    def far_rows(offset, to):
        parts = []
        for ref in col_refs:
            for j in range(nz):
                for core in range(2):
                    row = 2 * core * n_sum + offset
                    parts.append(ref[j, row : row + n_sum, to])
        return jnp.concatenate(parts, axis=0)

    def keep(i, to, b, value):
        if b < n_blocks:
            own_ref[i, blocks[b], here(to)] = value
        else:
            sent_ref[i, blocks[b - n_blocks], here(to)] = value

    def head(to):
        q, k_loc, v_loc, g = (
            jnp.concatenate([mine_ref[i, :, here(to)], came_ref[i, :, here(to)]], axis=0)
            for i in range(4)
        )
        k_far = far_rows(0, to)
        v_far = far_rows(n_sum, to)
        mask = near_mask[...]
        s_loc = jnp.concatenate([dot(q[b], k_loc[b], 1, 1) + mask for b in blocks], axis=0)
        s_far = dot(q, k_far, 1, 1) + away_mask[...]
        high = jnp.maximum(
            jnp.max(s_loc, axis=1, keepdims=True), jnp.max(s_far, axis=1, keepdims=True)
        )
        e_loc = jnp.exp2((s_loc - high) * exponent)
        e_far = jnp.exp2((s_far - high) * exponent)
        norm = jnp.sum(e_loc, axis=1, keepdims=True) + jnp.sum(e_far, axis=1, keepdims=True)
        inv = 1.0 / norm
        eb_loc = e_loc.astype(jnp.bfloat16)
        eb_far = e_far.astype(jnp.bfloat16)
        out = jnp.concatenate([dot(eb_loc[b], v_loc[b], 1, 0) for b in blocks], axis=0) + dot(
            eb_far, v_far, 1, 0
        )
        out = (out * inv).astype(jnp.bfloat16)
        gf = g.astype(jnp.float32)
        delta = jnp.sum(gf * out.astype(jnp.float32), axis=1, keepdims=True)
        factor = inv * scaling
        t_loc = jnp.concatenate([dot(g[b], v_loc[b], 1, 1) for b in blocks], axis=0)
        t_loc = (t_loc - delta) * factor
        t_far = (dot(g, v_far, 1, 1) - delta) * factor
        ds_loc = (eb_loc.astype(jnp.float32) * t_loc).astype(jnp.bfloat16)
        ds_far = (eb_far.astype(jnp.float32) * t_far).astype(jnp.bfloat16)
        dq = jnp.concatenate([dot(ds_loc[b], k_loc[b], 1, 0) for b in blocks], axis=0) + dot(
            ds_far, k_far, 1, 0
        )
        dq = dq.astype(jnp.bfloat16)
        gi = (gf * inv).astype(jnp.bfloat16)
        for n, b in enumerate(blocks):
            keep(0, to, n, out[b])
            keep(1, to, n, dq[b])
            for i, (left, right) in enumerate(((ds_loc, q), (eb_loc, gi))):
                part = dot(left[b], right[b], 0, 0)
                keep(2 + i, to, n, part.astype(jnp.bfloat16))
                t, row = n // n_blocks, (i * n_blocks + n % n_blocks) * EDGE
                near_ref[t, row : row + EDGE, to] = part[BLOCK - EDGE :, :]
        dk_far = dot(q, ds_far, 0, 0).astype(jnp.bfloat16).T
        dv_far = dot(gi, eb_far, 0, 0).astype(jnp.bfloat16).T
        row = 0
        for c in range(n_cols):
            for j in range(nz):
                ref, place = back_refs[c], j
                if c == n_cols - 1:
                    ref, place = back_refs[c + j % 2], j // 2
                for core in range(2):
                    to_row = 2 * core * n_sum
                    ref[place, to_row : to_row + n_sum, to] = dk_far[row : row + n_sum]
                    ref[place, to_row + n_sum : to_row + 2 * n_sum, to] = dv_far[row : row + n_sum]
                    row += n_sum

    def turn(step, carried):
        for u in range(unroll):
            h = step * unroll + u
            head(pl.ds(pl.multiple_of(h * HEAD_DIM, HEAD_DIM), HEAD_DIM))
        return carried

    lax.fori_loop(0, heads // unroll, turn, 0)


def attention(mine, came, mask, cols, earlier, after, first, heads):
    tokens = mine.shape[1]
    n_cols = len(cols)
    nz, rows, chunk_width = cols[0].shape
    n_sum = rows // 4
    nkeys = mask.shape[1]
    n_blocks = tokens // BLOCK
    results = jax.ShapeDtypeStruct(mine.shape, mine.dtype)
    near = jax.ShapeDtypeStruct((2, 2 * n_blocks * EDGE, chunk_width), jnp.float32)
    back = jax.ShapeDtypeStruct((nz, rows, chunk_width), jnp.bfloat16)
    half = jax.ShapeDtypeStruct((nz // 2, rows, chunk_width), jnp.bfloat16)
    n_skip = len(earlier) + len(after)
    return pl.pallas_call(
        functools.partial(attention_body, n_sum, n_cols, n_skip, first, heads),
        in_specs=[in_vmem] * (3 + n_cols + n_skip),
        out_specs=[in_vmem] * (4 + n_cols),
        out_shape=[results, results, near] + [back] * (n_cols - 1) + [half] * 2,
        scratch_shapes=[pltpu.VMEM((BLOCK, BLOCK), jnp.float32)],
        input_output_aliases={3 + n_cols + i: i for i in range(len(earlier))},
        compiler_params=params,
        cost_estimate=pl.CostEstimate(
            flops=heads * 24 * tokens * (BLOCK + nkeys) * HEAD_DIM,
            bytes_accessed=heads * HEAD_DIM * (32 * tokens + 8 * nkeys),
            transcendentals=heads * 2 * tokens * (BLOCK + nkeys),
        ),
        name="attention",
    )(mine, came, mask, *cols, *earlier, *after)


def hold_body(*refs):
    pass


def hold(arrays, *after):
    return pl.pallas_call(
        hold_body,
        in_specs=[in_vmem] * (len(arrays) + len(after)),
        out_specs=[in_vmem] * len(arrays),
        out_shape=[jax.ShapeDtypeStruct(a.shape, a.dtype) for a in arrays],
        input_output_aliases={i: i for i in range(len(arrays))},
        compiler_params=params,
        name="hold",
    )(*arrays, *after)


def line_body(at, n_far, own_ref, pair_ref, *refs):
    line_ref = refs[-1]
    line_ref[0] = own_ref[...]
    line_ref[1] = pair_ref[:, at : at + own_ref.shape[1]]
    for j in range(n_far):
        line_ref[2 + j] = refs[j][...]


def stack_line(own, pair, far, at, *after):
    return pl.pallas_call(
        functools.partial(line_body, at, len(far)),
        in_specs=[in_vmem] * (2 + len(far) + len(after)),
        out_specs=in_vmem,
        out_shape=jax.ShapeDtypeStruct((2 + len(far),) + own.shape, own.dtype),
        compiler_params=params,
        name="line",
    )(own, pair, *far, *after)


def pair_sum_body(keep_ref, came_ref, *refs):
    total = keep_ref[...].astype(jnp.float32) + came_ref[...].astype(jnp.float32)
    refs[-1][...] = total.astype(refs[-1].dtype)


def pair_sum(keep, came, *after):
    return pl.pallas_call(
        pair_sum_body,
        in_specs=[in_vmem] * (2 + len(after)),
        out_specs=in_vmem,
        out_shape=jax.ShapeDtypeStruct(keep.shape, keep.dtype),
        compiler_params=params,
        name="pair_sum",
    )(keep, came, *after)


def store_places(totals, out_refs, apart):
    if apart:
        for ref, total in zip(out_refs, totals):
            ref[...] = total.astype(ref.dtype)
        return
    for j, total in enumerate(totals):
        if j % 2 == 0:
            out_refs[j // 2][...] = total.astype(out_refs[j // 2].dtype)
        else:
            out_refs[-1][j // 2] = total.astype(out_refs[-1].dtype)


def places_shapes(n, rows, width, apart):
    kinds = [jnp.float32] + [jnp.bfloat16] * (n - 1)
    if apart:
        return [jax.ShapeDtypeStruct((rows, width), kind) for kind in kinds]
    shapes = [jax.ShapeDtypeStruct((rows, width), kind) for kind in kinds[0::2]]
    return shapes + [jax.ShapeDtypeStruct((n // 2, rows, width), jnp.bfloat16)]


def column_sum_body(n_in, n_after, apart, *refs):
    in_refs, out_refs = refs[:n_in], refs[n_in + n_after :]
    totals = []
    for j in range(in_refs[0].shape[0]):
        total = in_refs[0][j].astype(jnp.float32)
        for came in in_refs[1:-1]:
            total = total + came[j].astype(jnp.float32)
        if j % 2 == 0:
            total = total + in_refs[-1][j // 2].astype(jnp.float32)
        totals.append(total)
    store_places(totals, out_refs, apart)


def column_sum(parts, apart, *after):
    nz, rows, width = parts[0].shape
    shapes = places_shapes(nz, rows, width, apart)
    return pl.pallas_call(
        functools.partial(column_sum_body, len(parts), len(after), apart),
        in_specs=[in_vmem] * (len(parts) + len(after)),
        out_specs=[in_vmem] * len(shapes),
        out_shape=shapes,
        compiler_params=params,
        name="column_sum",
    )(*parts, *after)


def total_body(n, *refs):
    total = refs[0][...]
    for ref in refs[1:n]:
        total = total + ref[...].astype(jnp.float32)
    refs[-1][...] = total


def total_of(parts, *after):
    return pl.pallas_call(
        functools.partial(total_body, len(parts)),
        in_specs=[in_vmem] * (len(parts) + len(after)),
        out_specs=in_vmem,
        out_shape=jax.ShapeDtypeStruct(parts[0].shape, jnp.float32),
        compiler_params=params,
        name="total",
    )(*parts, *after)


def fold_body(n, *refs):
    keeps, came, out_refs = refs[:n], refs[n], refs[n + 1 :]
    totals = [
        keep[...].astype(jnp.float32) + came[i].astype(jnp.float32) for i, keep in enumerate(keeps)
    ]
    store_places(totals, out_refs, False)


def fold(keeps, came):
    n = len(keeps)
    shapes = places_shapes(n, *keeps[0].shape, False)
    return pl.pallas_call(
        functools.partial(fold_body, n),
        in_specs=[in_vmem] * (n + 1),
        out_specs=[in_vmem] * len(shapes),
        out_shape=shapes,
        compiler_params=params,
        name="fold",
    )(*keeps, came)


def edge_body(counts, *refs):
    targets = refs[-2:]
    at = 0
    start = 0
    for count in counts:
        near_ref, *ends = refs[start : start + count]
        start += count
        to = slice(at, at + near_ref.shape[2])
        at += near_ref.shape[2]
        total = ends[0][...]
        for term in ends[1:]:
            total = total + (term[0] if len(term.shape) == 3 else term[...]).astype(jnp.float32)
        rows = total.shape[0] // 2
        for t, target in enumerate(targets):
            for n in range(rows // SUMMARY):
                tile = near_ref[t, n * EDGE : (n + 1) * EDGE, :]
                more = total[t * rows + n * SUMMARY : t * rows + (n + 1) * SUMMARY]
                tile = [tile[: EDGE - SUMMARY], tile[EDGE - SUMMARY :] + more]
                tile = jnp.concatenate(tile, axis=0).astype(target.dtype)
                target[n * EDGE : (n + 1) * EDGE, to] = tile


def edge(chunks, *after):
    width = sum(chunk[0].shape[2] for chunk in chunks)
    shape = jax.ShapeDtypeStruct((chunks[0][0].shape[1], width), jnp.bfloat16)
    terms = [term for chunk in chunks for term in chunk]
    return pl.pallas_call(
        functools.partial(edge_body, [len(chunk) for chunk in chunks]),
        in_specs=[in_vmem] * (len(terms) + len(after)),
        out_specs=[in_vmem] * 2,
        out_shape=[shape] * 2,
        compiler_params=params,
        name="edge",
    )(*terms, *after)


def settle_body(place_ref, own_ref, came_ref, *refs):
    targets, (token_ref, sem) = refs[:4], refs[4:]
    half = own_ref.shape[2]
    copies = []
    for flip, source in enumerate((own_ref, came_ref)):
        to = core_window(place_ref, flip, half, 0, half)
        for i, target in enumerate(targets):
            copies.append(
                pltpu.make_async_copy(source.at[i], target.at[:, to], sem.at[flip, i])
            )
    for copy in copies:
        copy.start()
    token_ref[...] = jnp.zeros(token_ref.shape, token_ref.dtype)
    for copy in copies:
        copy.wait()


def settle(place, own, came):
    tokens, half = own.shape[1:]
    return pl.pallas_call(
        settle_body,
        in_specs=[in_smem, in_vmem, in_vmem],
        out_specs=[in_hbm] * 4 + [in_vmem],
        out_shape=[jax.ShapeDtypeStruct((tokens, 2 * half), own.dtype)] * 4
        + [jax.ShapeDtypeStruct((8, 128), jnp.float32)],
        scratch_shapes=[pltpu.SemaphoreType.DMA((2, 4))],
        compiler_params=params,
        name="settle",
    )(place, own, came)


def finish_body(n_edges, n_blocks, place_ref, *refs):
    edges = refs[2 : 2 + n_edges]
    targets, sem = refs[2 + n_edges : 4 + n_edges], refs[4 + n_edges]
    width = targets[0].shape[1]
    copies = []
    at = 0
    for e, source in enumerate(edges):
        flip = e % 2
        to = core_window(place_ref, flip, width // 2, at, source.shape[1])
        at += flip * source.shape[1]
        for n in range(2 * n_blocks):
            i, b = divmod(n, n_blocks)
            copies.append(
                pltpu.make_async_copy(
                    source.at[pl.ds(n * EDGE, EDGE)],
                    targets[i].at[pl.ds((b + 1) * BLOCK - EDGE, EDGE), to],
                    sem.at[e, n],
                )
            )
    for copy in copies:
        copy.start()
    for copy in copies:
        copy.wait()


def finish(place, dk, dv, edges):
    n_blocks = dk.shape[0] // BLOCK
    return pl.pallas_call(
        functools.partial(finish_body, len(edges), n_blocks),
        in_specs=[in_smem] + [in_hbm] * 2 + [in_vmem] * len(edges),
        out_specs=[in_hbm] * 2,
        out_shape=[jax.ShapeDtypeStruct(dk.shape, dk.dtype)] * 2,
        scratch_shapes=[pltpu.SemaphoreType.DMA((len(edges), 2 * n_blocks))],
        input_output_aliases={1: 0, 2: 1},
        compiler_params=params,
        name="finish",
    )(place, dk, dv, *edges)


def on_device(n_seq, nz, queries, keys_in, values_in, cotangent):
    n_cols = n_seq // 2
    n_chunks = len(chunk_heads)
    firsts = [sum(chunk_heads[:c]) for c in range(n_chunks)]

    def over_z(array, bits):
        return lax.ppermute(array, "head", [(i, i ^ bits) for i in range(nz)])

    def over_seq(array, bits):
        return lax.ppermute(array, "seq", [(i, i ^ bits) for i in range(n_seq)])

    def swap_far(pieces):
        return [over_z(pieces[j], j) for j in reversed(range(2, nz))][::-1]

    def swap_columns(parts):
        return [over_seq(parts[c], 2 * c) for c in reversed(range(1, len(parts)))][::-1]

    place = jnp.stack([lax.axis_index("seq"), lax.axis_index("head")]).astype(jnp.int32)
    arrays = (queries, keys_in, values_in, cotangent)
    mine = jnp.concatenate(summary_rows(keys_in) + summary_rows(values_in), axis=0)
    came = over_seq(mine, 1)
    part, side = away_heads(place, arrays, 0, queries.shape[1] // 2)
    pair = over_z(join(side, mine, came, 0, mine.shape[1] // 2), 1)
    ours, mask = stage(place, arrays, n_cols, nz)
    columns = []
    theirs = over_seq(hold([part], came)[0], 1)
    for c in range(n_chunks):
        width = chunk_heads[c] * HEAD_DIM
        at = firsts[c] * HEAD_DIM
        own = join(side, mine, came, at, width, *[cols[0] for cols in columns[-1:]])
        far = swap_far([own] * nz)
        line = stack_line(own, pair, far, at, *([cols[-1] for cols in columns[-1:]] or [theirs, mask]))
        columns.append([line] + swap_columns([line] * n_cols))

    results = ()
    chunks = []
    back = None
    for c in range(n_chunks):
        made = attention(
            ours,
            theirs,
            mask,
            columns[c],
            results,
            [cols[0] for cols in columns[c + 1 : c + 2]] + ([paired] if c else []),
            firsts[c],
            chunk_heads[c],
        )
        results, near, parts = made[:2], made[2], list(made[3:])
        waits = columns[c + 1] if c + 1 < n_chunks else [None] * n_cols
        if back is not None:
            waits = back[1]
        moved = [hold([parts[i]], waits[i])[0] for i in range(1, n_cols - 1)]
        give = hold([parts[n_cols]], waits[n_cols - 2])[0] if c else parts[n_cols]
        after = []
        if back is not None:
            *keeps, give_z = column_sum(back[1], False, near)
            after = keeps[:1]
        paired = pair_sum(parts[n_cols - 1], over_z(give, 1), *after)
        last = over_seq(paired, 2 * (n_cols - 1))
        moved = swap_columns(parts[:1] + moved) + [last]
        if back is not None:
            bits = 1
            while len(keeps) > 1:
                *keeps, give_z = fold(keeps, over_z(give_z, bits))
                bits *= 2
            chunks.append([back[0], keeps[0], over_z(give_z, bits)])
        back = near, parts[:1] + moved
    ends = column_sum(back[1], True, *chunks[-1][2:])
    pair, far = over_z(ends[1], 1), swap_far(ends)
    own, sent = results
    (sent,) = hold([sent], ends[0])
    *results, mark = settle(place, own, over_seq(sent, 1))
    chunks.append([back[0], total_of([ends[0]] + far, mark), pair])
    own, away = edge(chunks)
    attended, grad_queries, dk, dv = results
    edges = [own, over_seq(away, 1)]
    grad_keys, grad_values = finish(place, dk, dv, edges)
    return (attended, grad_queries, grad_keys, grad_values)


def solution(mesh):
    spec = P(("seq", "head"), None)
    return jax.shard_map(
        functools.partial(on_device, mesh.shape["seq"], mesh.shape["head"]),
        mesh=mesh,
        in_specs=(spec,) * 4,
        out_specs=(spec,) * 4,
        check_vma=False,
    )
```
